256 devices in a mesh: ctx: 16 (over x, y), head: 16 (over z, core).
Axes of the slice: x: 4, y: 4, z: 8, core: 2. Of those that a mesh axis runs over, the one named last changes fastest.
Arguments:
- queries: bfloat16 [4096, 64, 128], P('ctx', 'head'), may hold values from -1.75 to 1.75
- keys: bfloat16 [4096, 64, 128], P('ctx', 'head'), may hold values from -1.75 to 1.75
- values: bfloat16 [4096, 64, 128], P('ctx', 'head'), may hold values from -1.75 to 1.75
- out_weight: bfloat16 [8192, 6144], P('head'), may hold values from -0.0625 to 0.0625
- decay_rate: float32 [64], P('head'), may hold values from 4.8828124e-06 to 0.04
- out_grad: bfloat16 [4096, 6144], P(('ctx', 'head')), may hold values from -6 to 6
Outputs:
- layer_out: bfloat16 [4096, 6144], P(('ctx', 'head'))
- query_grad: bfloat16 [4096, 64, 128], P('ctx', 'head')
- key_grad: bfloat16 [4096, 64, 128], P('ctx', 'head')
- value_grad: bfloat16 [4096, 64, 128], P('ctx', 'head')
- weight_grad: float32 [8192, 6144], P('head', 'ctx')
The draws below stay inside these ranges and needn't reach their ends.
All inputs are finite; a program needn't handle non-finite values.
Results may differ from the reference program's by a relative error of at most 0.0057.
Values may be sent and summed in bfloat16 or wider, within the bound.
No kernel may reach another device: no remote copies, remote signals or barrier semaphores. Data moves between devices by JAX's collectives and lax.ppermute only.
A program may use at most 128 MiB of HBM per device.

```python
import math
import jax
import jax.numpy as jnp
from jax import lax

D = 6144
HEADS = 64
DH = 128
TOK_DEV = 256
TOKENS = 4096
N_CTX = 16


def strengthened(drawn, stream_key, source, target, shards_of, factor):
    owner, partner = [(jnp.arange(drawn.shape[axis_at]) // (drawn.shape[axis_at] // shards_of)).reshape([-1 if axis == axis_at else 1 for axis in range(drawn.ndim)]) for axis_at in (source, target)]
    chosen = jax.random.permutation(stream_key, shards_of)[partner]
    strong = (owner == chosen) | (owner == (partner + shards_of // 2) % shards_of)
    return jnp.where(strong, factor * drawn, drawn)


def shard_levels(rng, dims, cuts, least, top_value):
    loudness, own = 1.0, jax.random.fold_in(rng, 6)
    for axis_at, blocks in cuts:
        heights = jnp.exp(jax.random.uniform(jax.random.fold_in(own, axis_at), (blocks,), jnp.float32, least / len(cuts), top_value / len(cuts)))
        loudness = loudness * jnp.repeat(heights, dims[axis_at] // blocks).reshape([-1 if axis == axis_at else 1 for axis in range(len(dims))])
    return loudness


def gaussian(key, extent, width, reach, cuts=(), held_as=jnp.bfloat16):
    result = width * jax.random.normal(key, extent, jnp.float32)
    if cuts:
        result = result * shard_levels(key, extent, cuts, -0.22, 0.18)
    return jnp.clip(result, -reach, reach).astype(held_as)


def bell_draw_with(stream_key, dims, width, most, pieces, heavy, kind=jnp.bfloat16):
    entries = width * jax.random.normal(stream_key, dims, jnp.float32)
    if pieces:
        entries = entries * shard_levels(stream_key, dims, pieces, -0.22, 0.18)
    return jnp.clip(strengthened(entries, jax.random.fold_in(stream_key, 3), *heavy), -most, most).astype(kind)


def setup_inputs(seed: int = 0) -> dict:
    splits = jax.random.split(jax.random.key(seed), 7)
    queries = gaussian(splits[0], (TOKENS, HEADS, DH), (1.0 / (DH * TOKENS) ** 0.1667), 1.75, ((0, 16), (1, 16)))
    keys = gaussian(splits[1], (TOKENS, HEADS, DH), (1.0 / (DH * TOKENS) ** 0.1667), 1.75, ((0, 16), (1, 16)))
    values = gaussian(splits[2], (TOKENS, HEADS, DH), (1.0 / (DH * TOKENS) ** 0.1667), 1.75, ((0, 16), (1, 16)))
    out_weight = gaussian(splits[3], (HEADS * DH, D), (HEADS * DH) ** -0.5, 0.0625, ((0, 16),))
    decay_rate = jnp.clip(jnp.exp(math.log(0.04) - 9.010913 * jax.random.uniform(splits[4], (HEADS,), jnp.float32) ** shard_levels(splits[4], (HEADS,), ((0, 16),), -0.2, 0.2)), 4.882812390860636e-06, 0.04)
    out_grad = bell_draw_with(splits[5], (TOKENS, D), (1.0 / (DH * TOKENS) ** 0.1667), 6.0, ((0, 256),), (0, 1, 256, 6.0))
    return {"queries": queries, "keys": keys, "values": values, "out_weight": out_weight, "decay_rate": decay_rate, "out_grad": out_grad}


precise_mode = lax.Precision.HIGHEST


def rounded(array):
    return lax.optimization_barrier(array.astype(jnp.bfloat16)).astype(jnp.float32)


def product(form, left, right):
    return jnp.einsum(form, left, right, precision=precise_mode)


def reference(queries, keys, values, out_weight, decay_rate, out_grad):
    places = jnp.arange(TOK_DEV, dtype=jnp.float32)
    offsets = places[:, None] - places[None, :]
    mask_decay = jnp.where(offsets[None] >= 0, jnp.exp(-decay_rate[:, None, None] * jnp.maximum(offsets, 0.0)[None]), 0.0)
    end_weight = jnp.exp(-decay_rate[None, :] * (TOK_DEV - 1.0 - places)[:, None])
    start_weight = jnp.exp(-decay_rate[None, :] * places[:, None])
    inner_weight = jnp.exp(-decay_rate[None, :] * (places + 1.0)[:, None])
    tail_weight = jnp.exp(-decay_rate[None, :] * (TOK_DEV - places)[:, None])
    block_factor = jnp.exp(-decay_rate * TOK_DEV)
    block_shape = (N_CTX, TOK_DEV, HEADS, DH)
    query_blocks = queries.reshape(block_shape)
    key_blocks = keys.reshape(block_shape)
    value_blocks = values.reshape(block_shape)

    def forward_block(prev_state, inputs):
        query_wide = inputs[0].astype(jnp.float32)
        key_wide = inputs[1].astype(jnp.float32)
        value_wide = inputs[2].astype(jnp.float32)
        attn = rounded(product("thd,shd->hts", query_wide, key_wide) * mask_decay)
        inside = product("hts,she->the", attn, value_wide)
        outside = inner_weight[:, :, None] * product("thd,hde->the", query_wide, prev_state)
        keys_end = rounded(key_wide * end_weight[:, :, None])
        block_state = product("thd,the->hde", keys_end, value_wide)
        next_state = block_factor[:, None, None] * prev_state + block_state
        return next_state, (rounded(inside + outside), prev_state)

    zero_state = jnp.zeros((HEADS, DH, DH), jnp.float32)
    _, (attn_blocks, prev_states) = lax.scan(forward_block, zero_state, (query_blocks, key_blocks, value_blocks))
    flat_out = attn_blocks.reshape(TOKENS, HEADS * DH).astype(jnp.bfloat16)
    layer_out = jnp.dot(flat_out, out_weight, preferred_element_type=jnp.float32).astype(jnp.bfloat16)
    grad_flat = jnp.dot(out_grad, out_weight.T, preferred_element_type=jnp.float32).astype(jnp.bfloat16)
    weight_grad = jnp.dot(flat_out.T, out_grad, preferred_element_type=jnp.float32)
    grad_blocks = grad_flat.reshape(block_shape)

    def backward_block(next_grad, inputs):
        query_wide = inputs[0].astype(jnp.float32)
        key_wide = inputs[1].astype(jnp.float32)
        value_wide = inputs[2].astype(jnp.float32)
        grad_wide = inputs[3].astype(jnp.float32)
        prev_state = inputs[4]
        attn = rounded(product("thd,shd->hts", query_wide, key_wide) * mask_decay)
        queries_start = rounded(query_wide * start_weight[:, :, None])
        grad_block = product("thd,the->hde", queries_start, grad_wide)
        grad_scores = rounded(product("the,she->hts", grad_wide, value_wide) * mask_decay)
        query_grad = product("hts,shd->thd", grad_scores, key_wide) + inner_weight[:, :, None] * product("the,hde->thd", grad_wide, prev_state)
        key_grad = product("hts,thd->shd", grad_scores, query_wide) + tail_weight[:, :, None] * product("she,hde->shd", value_wide, next_grad)
        value_grad = product("hts,the->she", attn, grad_wide) + tail_weight[:, :, None] * product("shd,hde->she", key_wide, next_grad)
        carried = block_factor[:, None, None] * next_grad + grad_block
        return carried, (query_grad.astype(jnp.bfloat16), key_grad.astype(jnp.bfloat16), value_grad.astype(jnp.bfloat16))

    _, (query_grads, key_grads, value_grads) = lax.scan(backward_block, zero_state, (query_blocks, key_blocks, value_blocks, grad_blocks, prev_states), reverse=True)
    full_shape = (TOKENS, HEADS, DH)
    return (layer_out, query_grads.reshape(full_shape), key_grads.reshape(full_shape), value_grads.reshape(full_shape), weight_grad)
```

```python
import jax
import jax.numpy as jnp
from jax import lax
from jax.experimental import pallas as pl
from jax.experimental.pallas import tpu as pltpu
from jax.sharding import PartitionSpec as P

F32 = jnp.float32
BF16 = jnp.bfloat16
N_CTX = 16
N_Z = 8

CORE_PAIR = [(h, h ^ 1) for h in range(16)]
ORDERS = ((1, 3, 4, 12), (3, 1, 12, 4), (4, 12, 1, 3), (12, 4, 3, 1))


def z_shift(d):
    return [(h, (h + 2 * d) % 16) for h in range(16)]


def x_shift(d):
    return [(c, (c + 4 * d) % 16) for c in range(16)]


def y_shift(d):
    return [(c, (c // 4) * 4 + (c + d) % 4) for c in range(16)]


def xor_pairs(mask):
    return [(c, c ^ mask) for c in range(16)]


def gather_masks(order):
    masks = [0]
    for mask in order:
        masks = masks + [m ^ mask for m in masks]
    return masks


def two_level_sum(state, rate, length, reverse):
    place = lax.axis_index("ctx")
    x, y = place // 4, place % 4
    sign = -1 if reverse else 1

    def power(n):
        return jnp.exp(-rate * (length * n.astype(F32)))[:, None, None]

    def ahead(at, d):
        return (at >= d) if not reverse else (at + d <= 3)

    def level(own, at, shift, scale):
        sent = own.astype(BF16)
        got = [lax.ppermute(sent, "ctx", shift(sign * d)).astype(F32) for d in (1, 2, 3)]
        before = 0.0
        for d in (1, 2, 3):
            weight = jnp.where(ahead(at, d), power(jnp.asarray((d - 1) * scale)), 0.0)
            before = before + weight * got[d - 1]
        return before, got

    before_y, got = level(state, y, y_shift, 1)
    to_end = (3 - y) if not reverse else y
    total = power(to_end) * state
    for d in (1, 2, 3):
        source = (y - sign * d) % 4
        left = (3 - source) if not reverse else source
        total = total + power(left) * got[d - 1]
    before_x, _ = level(total, x, x_shift, 4)
    steps = y if not reverse else 3 - y
    return before_y + power(steps) * before_x


def weight_kernel(first, orders, *refs):
    parts = refs[:4]
    cols = refs[4]
    out = refs[-1]
    for j in range(4):
        total = jnp.zeros((128, 384), F32) if first else refs[5][j * 128 : (j + 1) * 128, :]
        for i in range(8):
            block = cols[:, orders[j][i]].reshape(256, 384)
            total = total + lax.dot_general(
                parts[j][i * 256 : (i + 1) * 256, :],
                block,
                (((0,), (0,)), ((), ())),
                preferred_element_type=F32,
            )
        out[j * 128 : (j + 1) * 128, :] = total


def weight_product(parts, cols, orders, earlier):
    first = earlier is None
    operands = list(parts) + [cols] + ([] if first else [earlier])
    return pl.pallas_call(
        lambda *refs: weight_kernel(first, orders, *refs),
        out_shape=jax.ShapeDtypeStruct((512, 384), F32),
        in_specs=[pl.BlockSpec(memory_space=pltpu.VMEM)] * len(operands),
        out_specs=pl.BlockSpec(memory_space=pltpu.VMEM),
        compiler_params=pltpu.CompilerParams(vmem_limit_bytes=32 * 2**20),
        cost_estimate=pl.CostEstimate(
            flops=2 * 2048 * 512 * 384, bytes_accessed=6 * 2**20, transcendentals=0
        ),
    )(*operands)


def body(queries, keys, values, out_weight, decay_rate, out_grad):
    length, heads_here, head_size = queries.shape
    ctx = lax.axis_index("ctx")
    head = lax.axis_index("head")
    z, core = head // 2, head % 2
    n_col = out_grad.shape[1] // N_CTX

    forward = backward = out_grad
    relative = {0: out_grad}
    for s in range(1, 5):
        forward = lax.ppermute(forward, "head", z_shift(1))
        relative[(-s) % 8] = forward
        if s < 4:
            backward = lax.ppermute(backward, "head", z_shift(-1))
            relative[s] = backward
    rows_here = jnp.concatenate([relative[k] for k in range(8)], axis=0)
    rows_there = lax.ppermute(rows_here, "head", CORE_PAIR)

    mine = lax.all_to_all(
        out_grad.reshape(16, N_CTX, n_col), "ctx", split_axis=1, concat_axis=0, tiled=False
    )
    mine = jnp.take(mine, ctx ^ jnp.arange(16), axis=0)
    cols = lax.all_gather(mine, "head", axis=0)

    places = jnp.arange(length, dtype=F32)
    offsets = places[:, None] - places[None, :]
    mask_decay = jnp.where(
        offsets[None] >= 0,
        jnp.exp(-decay_rate[:, None, None] * jnp.maximum(offsets, 0.0)[None]),
        0.0,
    )

    def decay(n):
        return jnp.exp(-decay_rate[:, None] * n[None, :])[:, :, None]

    end_weight = decay(length - 1.0 - places)
    start_weight = decay(places)
    inner_weight = decay(places + 1.0)
    tail_weight = decay(length - places)

    q = jnp.transpose(queries, (1, 0, 2))
    k = jnp.transpose(keys, (1, 0, 2))
    v = jnp.transpose(values, (1, 0, 2))

    def mm(form, a, b):
        return jnp.einsum(form, a, b, preferred_element_type=F32)

    keys_end = (k * end_weight).astype(BF16)
    block_state = mm("htd,hte->hde", keys_end, v)
    prev_state = two_level_sum(block_state, decay_rate, float(length), False).astype(BF16)
    attn = (mm("htd,hsd->hts", q, k) * mask_decay).astype(BF16)
    inside = mm("hts,hse->hte", attn, v)
    attn_out = (inside + inner_weight * mm("htd,hde->hte", q, prev_state)).astype(BF16)

    held = [attn_out[j] for j in range(4)]
    for step in range(3):
        got = [
            lax.ppermute(held[j], "ctx", xor_pairs(ORDERS[j][step])) for j in range(4)
        ]
        held = [jnp.concatenate([held[j], got[j]], axis=0) for j in range(4)]
    last = [lax.ppermute(held[j], "ctx", xor_pairs(ORDERS[j][3])) for j in range(4)]

    flat_out = jnp.transpose(attn_out, (1, 0, 2)).reshape(length, heads_here * head_size)
    flat_out = flat_out.reshape(N_Z, 2, 16, heads_here * head_size)
    theirs = lax.dynamic_index_in_dim(flat_out, 1 - core, 1, keepdims=False).reshape(128, -1)
    ours = lax.dynamic_index_in_dim(flat_out, core, 1, keepdims=False).reshape(128, -1)
    part_theirs = jnp.dot(theirs, out_weight, preferred_element_type=F32).astype(BF16)
    from_pair = lax.ppermute(part_theirs, "head", CORE_PAIR)
    part = jnp.dot(ours, out_weight, preferred_element_type=F32) + from_pair.astype(F32)
    part = part.reshape(N_Z, 16, -1)

    def piece(d):
        return lax.dynamic_index_in_dim(part, (z + d) % 8, 0, keepdims=False)

    up = lax.ppermute(piece(4).astype(BF16), "head", z_shift(1))
    down = lax.ppermute(piece(-3).astype(BF16), "head", z_shift(-1))
    for s in (3, 2, 1):
        up = lax.ppermute((up.astype(F32) + piece(s)).astype(BF16), "head", z_shift(1))
        if s < 3:
            down = lax.ppermute((down.astype(F32) + piece(-s)).astype(BF16), "head", z_shift(-1))
    layer_out = (piece(0) + up.astype(F32) + down.astype(F32)).astype(BF16)

    rows = jnp.concatenate([rows_here, rows_there], axis=0)
    grad_rot = lax.dot_general(
        rows, out_weight, (((1,), (1,)), ((), ())), preferred_element_type=F32
    ).astype(BF16)
    grad_rot = grad_rot.reshape(2, N_Z, 16, heads_here * head_size)
    grad_rot = jnp.roll(grad_rot, z, axis=1)
    grad_rot = jnp.where(core == 0, grad_rot, grad_rot[::-1])
    g = jnp.transpose(
        grad_rot.reshape(2, N_Z, 16, heads_here, head_size), (3, 1, 0, 2, 4)
    ).reshape(heads_here, length, head_size)

    queries_start = (q * start_weight).astype(BF16)
    grad_block = mm("htd,hte->hde", queries_start, g)
    next_grad = two_level_sum(grad_block, decay_rate, float(length), True).astype(BF16)
    grad_scores = (mm("hte,hse->hts", g, v) * mask_decay).astype(BF16)
    query_grad = mm("hts,hsd->htd", grad_scores, k) + inner_weight * mm(
        "hte,hde->htd", g, prev_state
    )
    key_grad = mm("hts,htd->hsd", grad_scores, q) + tail_weight * mm(
        "hse,hde->hsd", v, next_grad
    )
    value_grad = mm("hts,hte->hse", attn, g) + tail_weight * mm(
        "hsd,hde->hse", k, next_grad
    )

    masks = [gather_masks(order) for order in ORDERS]
    weight_grad = weight_product(held, cols, [m[:8] for m in masks], None)
    weight_grad = weight_product(last, cols, [m[8:] for m in masks], weight_grad)

    def back(a):
        return jnp.transpose(a, (1, 0, 2)).astype(BF16)

    return (layer_out, back(query_grad), back(key_grad), back(value_grad), weight_grad)


def solution(mesh):
    return jax.shard_map(
        body,
        mesh=mesh,
        in_specs=(
            P("ctx", "head", None),
            P("ctx", "head", None),
            P("ctx", "head", None),
            P("head", None),
            P("head"),
            P(("ctx", "head"), None),
        ),
        out_specs=(
            P(("ctx", "head"), None),
            P("ctx", "head", None),
            P("ctx", "head", None),
            P("ctx", "head", None),
            P("head", "ctx"),
        ),
        check_vma=False,
    )
```

```python
import jax
import jax.numpy as jnp
from jax import lax
from jax.experimental import pallas as pl
from jax.experimental.pallas import tpu as pltpu
from jax.sharding import PartitionSpec as P

F32 = jnp.float32
BF16 = jnp.bfloat16
N_CTX = 16
N_Z = 8

CORE_PAIR = [(h, h ^ 1) for h in range(16)]
SPREAD = [(h, (h - 2 if h % 2 == 0 else h + 2) % 16) for h in range(16)]
COLLECT = [(h, (h + 2 if h % 2 == 0 else h - 2) % 16) for h in range(16)]
ORDERS = (((1, 3, 4, 12), (4, 12, 1, 3)), ((3, 1, 12, 4), (12, 4, 3, 1)))


def x_shift(d):
    return [(c, (c + 4 * d) % 16) for c in range(16)]


def y_shift(d):
    return [(c, (c // 4) * 4 + (c + d) % 4) for c in range(16)]


def step_pairs(pair, step):
    masks = [ORDERS[pair][core][step] for core in range(2)]
    return [
        (c * 16 + h, (c ^ masks[h % 2]) * 16 + h) for c in range(16) for h in range(16)
    ]


def gather_masks(order):
    masks = [0]
    for mask in order:
        masks = masks + [m ^ mask for m in masks]
    return masks


def two_level_sum(state, rate, length, reverse):
    place = lax.axis_index("ctx")
    x, y = place // 4, place % 4
    sign = -1 if reverse else 1

    def power(n):
        return jnp.exp(-rate * (length * n.astype(F32)))[:, None, None]

    def ahead(at, d):
        return (at >= d) if not reverse else (at + d <= 3)

    def level(own, at, shift, scale):
        sent = own.astype(BF16)
        got = [lax.ppermute(sent, "ctx", shift(sign * d)).astype(F32) for d in (1, 2, 3)]
        before = 0.0
        for d in (1, 2, 3):
            weight = jnp.where(ahead(at, d), power(jnp.asarray((d - 1) * scale)), 0.0)
            before = before + weight * got[d - 1]
        return before, got

    before_y, got = level(state, y, y_shift, 1)
    to_end = (3 - y) if not reverse else y
    total = power(to_end) * state
    for d in (1, 2, 3):
        source = (y - sign * d) % 4
        left = (3 - source) if not reverse else source
        total = total + power(left) * got[d - 1]
    before_x, _ = level(total, x, x_shift, 4)
    steps = y if not reverse else 3 - y
    return before_y + power(steps) * before_x


def weight_kernel(first, table, a0, a1, ours, theirs, *refs):
    out = refs[-1]
    for pair, part in enumerate((a0, a1)):
        rows = slice(pair * 256, (pair + 1) * 256)
        total = jnp.zeros((256, 384), F32) if first else refs[0][rows, :]
        for i in range(8):
            at = table[pair, i]
            block = jnp.concatenate([ours[at], theirs[at]], axis=0)
            total = total + lax.dot_general(
                part[i * 256 : (i + 1) * 256, :],
                block,
                (((0,), (0,)), ((), ())),
                preferred_element_type=F32,
            )
        out[rows, :] = total


def weight_product(table, parts, ours, theirs, earlier):
    first = earlier is None
    operands = list(parts) + [ours, theirs] + ([] if first else [earlier])
    return pl.pallas_call(
        lambda *refs: weight_kernel(first, *refs),
        out_shape=jax.ShapeDtypeStruct((512, 384), F32),
        in_specs=[pl.BlockSpec(memory_space=pltpu.SMEM)]
        + [pl.BlockSpec(memory_space=pltpu.VMEM)] * len(operands),
        out_specs=pl.BlockSpec(memory_space=pltpu.VMEM),
        compiler_params=pltpu.CompilerParams(vmem_limit_bytes=32 * 2**20),
        cost_estimate=pl.CostEstimate(
            flops=2 * 2048 * 512 * 384, bytes_accessed=6 * 2**20, transcendentals=0
        ),
    )(table, *operands)


def body(queries, keys, values, out_weight, decay_rate, out_grad):
    length, heads_here, head_size = queries.shape
    ctx = lax.axis_index("ctx")
    head = lax.axis_index("head")
    z, core = head // 2, head % 2
    n_col = out_grad.shape[1] // N_CTX

    sign = 1 - 2 * core

    def swap(a):
        return lax.ppermute(a, "head", CORE_PAIR)

    def half_order(of_core, s):
        pieces = []
        for k in (1, 2, 3):
            base = 2 * ((z + s * k) % 8)
            pieces += [base, base + 1]
        return pieces + [2 * ((z + 4) % 8) + of_core, 2 * z + of_core]

    order = jnp.stack(half_order(core, sign) + half_order(1 - core, -sign))
    back_order = jnp.sum(
        jnp.where(order[:, None] == jnp.arange(16)[None, :], jnp.arange(16)[:, None], 0), axis=0
    )

    def reorder(a, by):
        return jnp.take(a.reshape(16, 16, -1), by, axis=0, mode="clip").reshape(a.shape)

    other = swap(out_grad)
    chunk = jnp.where(
        core == 0,
        jnp.concatenate([out_grad, other], axis=0),
        jnp.concatenate([other, out_grad], axis=0),
    )
    chunks = []
    for k in (1, 2, 3):
        chunk = lax.ppermute(chunk, "head", SPREAD)
        chunks.append(chunk)
    early = jnp.concatenate(chunks[:2], axis=0)
    early_there = swap(early)
    quarter = lax.dynamic_slice_in_dim(chunk, core * 16, 16, axis=0)
    quarter = lax.ppermute(quarter, "head", SPREAD)
    late = jnp.concatenate([chunks[2], quarter], axis=0)
    late_there = swap(late)
    rows_here = jnp.concatenate([early, late, out_grad], axis=0)
    rows = jnp.concatenate([rows_here, early_there, late_there, other], axis=0)

    cols_here = lax.all_to_all(
        jnp.transpose(rows_here.reshape(128, N_CTX, n_col), (1, 0, 2)),
        "ctx",
        split_axis=0,
        concat_axis=0,
        tiled=True,
    )
    cols_there = swap(cols_here)

    places = jnp.arange(length, dtype=F32)
    offsets = places[:, None] - places[None, :]
    mask_decay = jnp.where(
        offsets[None] >= 0,
        jnp.exp(-decay_rate[:, None, None] * jnp.maximum(offsets, 0.0)[None]),
        0.0,
    )

    def decay(n):
        return jnp.exp(-decay_rate[:, None] * n[None, :])[:, :, None]

    end_weight = decay(length - 1.0 - places)
    start_weight = decay(places)
    inner_weight = decay(places + 1.0)
    tail_weight = decay(length - places)

    q = jnp.transpose(queries, (1, 0, 2))
    k = jnp.transpose(keys, (1, 0, 2))
    v = jnp.transpose(values, (1, 0, 2))

    def mm(form, a, b):
        return jnp.einsum(form, a, b, preferred_element_type=F32)

    def split(a):
        high = a.astype(BF16)
        return high, (a - high.astype(F32)).astype(BF16)

    def mm_split(form, a, b):
        return mm(form, a, b[0]) + mm(form, a, b[1])

    keys_end = (k * end_weight).astype(BF16)
    block_state = mm("htd,hte->hde", keys_end, v)
    prev_state = split(two_level_sum(block_state, decay_rate, float(length), False))
    attn = (mm("htd,hsd->hts", q, k) * mask_decay).astype(BF16)
    inside = mm("hts,hse->hte", attn, v)
    attn_out = (inside + inner_weight * mm_split("htd,hde->hte", q, prev_state)).astype(BF16)

    flat_out = jnp.transpose(attn_out, (1, 0, 2)).reshape(length, heads_here * head_size)
    flat_out = reorder(flat_out, order)

    part_there = jnp.dot(flat_out[128:], out_weight, preferred_element_type=F32)
    from_pair = swap(part_there.astype(BF16))
    part = jnp.dot(flat_out[:128], out_weight, preferred_element_type=F32)
    part = part + from_pair.astype(F32)

    held = [flat_out[:, :256], flat_out[:, 256:]]
    for step in range(3):
        got = [
            lax.ppermute(held[p], ("ctx", "head"), step_pairs(p, step)) for p in range(2)
        ]
        held = [jnp.concatenate([held[p], got[p]], axis=0) for p in range(2)]
    last = [lax.ppermute(held[p], ("ctx", "head"), step_pairs(p, 3)) for p in range(2)]

    moving = lax.ppermute(part[96:112].astype(BF16), "head", COLLECT).astype(F32)
    zero = jnp.zeros_like(moving)
    moving = jnp.where(
        core == 0,
        jnp.concatenate([moving, zero], axis=0),
        jnp.concatenate([zero, moving], axis=0),
    )
    for at in (64, 32, 0):
        moving = (moving + part[at : at + 32]).astype(BF16)
        moving = lax.ppermute(moving, "head", COLLECT).astype(F32)
    moving = moving.astype(BF16)
    for_here = lax.dynamic_slice_in_dim(moving, core * 16, 16, axis=0)
    for_there = lax.dynamic_slice_in_dim(moving, (1 - core) * 16, 16, axis=0)
    layer_out = part[112:128] + for_here.astype(F32) + swap(for_there).astype(F32)
    layer_out = layer_out.astype(BF16)

    grad_flat = lax.dot_general(
        rows, out_weight, (((1,), (1,)), ((), ())), preferred_element_type=F32
    ).astype(BF16)
    grad_flat = reorder(grad_flat, back_order)
    g = jnp.transpose(grad_flat.reshape(length, heads_here, head_size), (1, 0, 2))

    queries_start = (q * start_weight).astype(BF16)
    grad_block = mm("htd,hte->hde", queries_start, g)
    next_grad = split(two_level_sum(grad_block, decay_rate, float(length), True))
    grad_scores = (mm("hte,hse->hts", g, v) * mask_decay).astype(BF16)
    query_grad = mm("hts,hsd->htd", grad_scores, k) + inner_weight * mm_split(
        "hte,hde->htd", g, prev_state
    )
    key_grad = mm("hts,htd->hsd", grad_scores, q) + tail_weight * mm_split(
        "hse,hde->hsd", v, next_grad
    )
    value_grad = mm("hts,hte->hse", attn, g) + tail_weight * mm_split(
        "hsd,hde->hse", k, next_grad
    )

    masks = jnp.asarray(
        [[gather_masks(ORDERS[p][c]) for p in range(2)] for c in range(2)], jnp.int32
    )
    table = ctx.astype(jnp.int32) ^ jnp.where(core == 0, masks[0], masks[1])
    weight_grad = weight_product(table[:, :8], held, cols_here, cols_there, None)
    weight_grad = weight_product(table[:, 8:], last, cols_here, cols_there, weight_grad)

    def back(a):
        return jnp.transpose(a, (1, 0, 2)).astype(BF16)

    return (layer_out, back(query_grad), back(key_grad), back(value_grad), weight_grad)


def solution(mesh):
    return jax.shard_map(
        body,
        mesh=mesh,
        in_specs=(
            P("ctx", "head", None),
            P("ctx", "head", None),
            P("ctx", "head", None),
            P("head", None),
            P("head"),
            P(("ctx", "head"), None),
        ),
        out_specs=(
            P(("ctx", "head"), None),
            P("ctx", "head", None),
            P("ctx", "head", None),
            P("ctx", "head", None),
            P("head", "ctx"),
        ),
        check_vma=False,
    )
```

```python
import jax
import jax.numpy as jnp
from jax import lax
from jax.experimental import pallas as pl
from jax.experimental.pallas import tpu as pltpu
from jax.sharding import PartitionSpec as P

F32 = jnp.float32
BF16 = jnp.bfloat16
N_CTX = 16
N_Z = 8

CORE_PAIR = [(h, h ^ 1) for h in range(16)]
SPREAD = [(h, (h - 2 if h % 2 == 0 else h + 2) % 16) for h in range(16)]
COLLECT = [(h, (h + 2 if h % 2 == 0 else h - 2) % 16) for h in range(16)]
ORDERS = (((1, 3, 4, 12), (4, 12, 1, 3)), ((3, 1, 12, 4), (12, 4, 3, 1)))


def x_shift(d):
    return [(c, (c + 4 * d) % 16) for c in range(16)]


def y_shift(d):
    return [(c, (c // 4) * 4 + (c + d) % 4) for c in range(16)]


def step_pairs(pair, step):
    masks = [ORDERS[pair][core][step] for core in range(2)]
    return [
        (c * 16 + h, (c ^ masks[h % 2]) * 16 + h) for c in range(16) for h in range(16)
    ]


def gather_masks(order):
    masks = [0]
    for mask in order:
        masks = masks + [m ^ mask for m in masks]
    return masks


def two_level_sum(state, rate, length, reverse, ties):
    place = lax.axis_index("ctx")
    x, y = place // 4, place % 4
    sign = -1 if reverse else 1

    def power(n):
        return jnp.exp(-rate * (length * n.astype(F32)))[:, None, None]

    def ahead(at, d):
        return (at >= d) if not reverse else (at + d <= 3)

    def level(own, at, shift, scale, tie):
        sent = own.astype(BF16)
        got = [lax.ppermute(sent, "ctx", shift(sign * d)) for d in (1, 2, 3)]
        if tie is not None:
            got = lax.optimization_barrier((*got, tie))[:3]
        got = [part.astype(F32) for part in got]
        before = 0.0
        for d in (1, 2, 3):
            weight = jnp.where(ahead(at, d), power(jnp.asarray((d - 1) * scale)), 0.0)
            before = before + weight * got[d - 1]
        return before, got

    before_y, got = level(state, y, y_shift, 1, ties[0])
    to_end = (3 - y) if not reverse else y
    total = power(to_end) * state
    for d in (1, 2, 3):
        source = (y - sign * d) % 4
        left = (3 - source) if not reverse else source
        total = total + power(left) * got[d - 1]
    before_x, _ = level(total, x, x_shift, 4, ties[1])
    steps = y if not reverse else 3 - y
    return before_y + power(steps) * before_x


def weight_kernel(first, table, a0, a1, ours, theirs, *refs):
    out = refs[-1]
    for pair, part in enumerate((a0, a1)):
        rows = slice(pair * 256, (pair + 1) * 256)
        total = jnp.zeros((256, 384), F32) if first else refs[0][rows, :]
        for i in range(8):
            at = table[pair, i]
            block = jnp.concatenate([ours[at], theirs[at]], axis=0)
            total = total + lax.dot_general(
                part[i * 256 : (i + 1) * 256, :],
                block,
                (((0,), (0,)), ((), ())),
                preferred_element_type=F32,
            )
        out[rows, :] = total


def weight_product(table, parts, ours, theirs, earlier):
    first = earlier is None
    operands = list(parts) + [ours, theirs] + ([] if first else [earlier])
    return pl.pallas_call(
        lambda *refs: weight_kernel(first, *refs),
        out_shape=jax.ShapeDtypeStruct((512, 384), F32),
        in_specs=[pl.BlockSpec(memory_space=pltpu.SMEM)]
        + [pl.BlockSpec(memory_space=pltpu.VMEM)] * len(operands),
        out_specs=pl.BlockSpec(memory_space=pltpu.VMEM),
        compiler_params=pltpu.CompilerParams(vmem_limit_bytes=32 * 2**20),
        cost_estimate=pl.CostEstimate(
            flops=2 * 2048 * 512 * 384, bytes_accessed=6 * 2**20, transcendentals=0
        ),
    )(table, *operands)


def pack_kernel(c1, c2, c3, quarter, own, out):
    n_col = out.shape[2]
    row = 0
    for part in (c1, c2, c3, quarter, own):
        size = part.shape[0]
        for c in range(out.shape[0]):
            out[c, row : row + size, :] = part[:, c * n_col : (c + 1) * n_col]
        row += size


def pack_columns(parts, n_col):
    return pl.pallas_call(
        pack_kernel,
        out_shape=jax.ShapeDtypeStruct((N_CTX, 128, n_col), BF16),
        in_specs=[pl.BlockSpec(memory_space=pltpu.VMEM)] * 5,
        out_specs=pl.BlockSpec(memory_space=pltpu.VMEM),
        compiler_params=pltpu.CompilerParams(vmem_limit_bytes=16 * 2**20),
        cost_estimate=pl.CostEstimate(flops=0, bytes_accessed=3 * 2**20, transcendentals=0),
    )(*parts)


def grad_kernel(order, ours, theirs, weight, out, total):
    step = pl.program_id(0)

    @pl.when(step == 0)
    def _():
        total[...] = jnp.zeros_like(total)

    n_col = ours.shape[2]
    for c in range(ours.shape[0]):
        total[...] += lax.dot_general(
            jnp.concatenate([ours[c], theirs[c]], axis=0),
            weight[:, c * n_col : (c + 1) * n_col],
            (((1,), (1,)), ((), ())),
            preferred_element_type=F32,
        )

    @pl.when(step == pl.num_programs(0) - 1)
    def _():
        for piece in range(16):
            to = pl.ds(pl.multiple_of(order[piece] * 16, 16), 16)
            rows = total[piece * 16 : (piece + 1) * 16, :].astype(BF16)
            for j in range(4):
                out[j, to, :] = rows[:, j * 128 : (j + 1) * 128]


def grad_product(order, ours, theirs, weight):
    n_col = ours.shape[2]
    rows_spec = pl.BlockSpec((4, 128, n_col), lambda i: (i, 0, 0))
    return pl.pallas_call(
        grad_kernel,
        out_shape=jax.ShapeDtypeStruct((4, 256, 128), BF16),
        grid=(4,),
        in_specs=[pl.BlockSpec(memory_space=pltpu.SMEM), rows_spec, rows_spec, pl.BlockSpec((512, 4 * n_col), lambda i: (0, i))],
        out_specs=pl.BlockSpec((4, 256, 128), lambda i: (0, 0, 0)),
        scratch_shapes=[pltpu.VMEM((256, 512), F32)],
        compiler_params=pltpu.CompilerParams(vmem_limit_bytes=58 * 2**20),
        cost_estimate=pl.CostEstimate(
            flops=2 * 256 * 512 * 6144, bytes_accessed=10 * 2**20, transcendentals=0
        ),
    )(order, ours, theirs, weight)


def layer_kernel(flat, weight, ours, theirs):
    both = jnp.dot(flat[...], weight[...], preferred_element_type=F32)
    ours[...] = both[:128]
    theirs[...] = both[128:].astype(BF16)


def layer_product(flat, weight):
    width = weight.shape[1] // 4
    return pl.pallas_call(
        layer_kernel,
        out_shape=(
            jax.ShapeDtypeStruct((128, 4 * width), F32),
            jax.ShapeDtypeStruct((128, 4 * width), BF16),
        ),
        grid=(4,),
        in_specs=[
            pl.BlockSpec((256, 512), lambda i: (0, 0)),
            pl.BlockSpec((512, width), lambda i: (0, i)),
        ],
        out_specs=(
            pl.BlockSpec((128, width), lambda i: (0, i)),
            pl.BlockSpec((128, width), lambda i: (0, i)),
        ),
        compiler_params=pltpu.CompilerParams(vmem_limit_bytes=58 * 2**20),
        cost_estimate=pl.CostEstimate(
            flops=2 * 256 * 512 * 6144, bytes_accessed=11 * 2**20, transcendentals=0
        ),
    )(flat, weight)


def body(queries, keys, values, out_weight, decay_rate, out_grad):
    length, heads_here, head_size = queries.shape
    ctx = lax.axis_index("ctx")
    head = lax.axis_index("head")
    z, core = head // 2, head % 2
    n_col = out_grad.shape[1] // N_CTX

    sign = 1 - 2 * core

    def swap(a):
        return lax.ppermute(a, "head", CORE_PAIR)

    def half_order(of_core, s):
        pieces = []
        for k in (1, 2, 3):
            base = 2 * ((z + s * k) % 8)
            pieces += [base, base + 1]
        return pieces + [2 * ((z + 4) % 8) + of_core, 2 * z + of_core]

    order = jnp.stack(half_order(core, sign) + half_order(1 - core, -sign))
    def reorder(a, by):
        return jnp.take(a.reshape(16, 16, -1), by, axis=0, mode="clip").reshape(a.shape)

    other = swap(out_grad)
    chunk = jnp.where(
        core == 0,
        jnp.concatenate([out_grad, other], axis=0),
        jnp.concatenate([other, out_grad], axis=0),
    )
    chunk_first = chunk
    chunks = []
    for k in (1, 2, 3):
        chunk = lax.ppermute(chunk, "head", SPREAD)
        chunks.append(chunk)
    quarter = lax.dynamic_slice_in_dim(chunk, core * 16, 16, axis=0)
    quarter = lax.ppermute(quarter, "head", SPREAD)

    packed = pack_columns((*chunks, quarter, out_grad), n_col)
    packed_there = swap(packed)
    cols_here = lax.all_to_all(packed, "ctx", split_axis=0, concat_axis=0, tiled=True)
    places = jnp.arange(length, dtype=F32)
    offsets = places[:, None] - places[None, :]
    mask_decay = jnp.where(
        offsets[None] >= 0,
        jnp.exp(-decay_rate[:, None, None] * jnp.maximum(offsets, 0.0)[None]),
        0.0,
    )

    def decay(n):
        return jnp.exp(-decay_rate[:, None] * n[None, :])[:, :, None]

    end_weight = decay(length - 1.0 - places)
    start_weight = decay(places)
    inner_weight = decay(places + 1.0)
    tail_weight = decay(length - places)

    q = jnp.transpose(queries, (1, 0, 2))
    k = jnp.transpose(keys, (1, 0, 2))
    v = jnp.transpose(values, (1, 0, 2))

    def mm(form, a, b):
        return jnp.einsum(form, a, b, preferred_element_type=F32)

    def split(a):
        high = a.astype(BF16)
        return high, (a - high.astype(F32)).astype(BF16)

    def mm_split(form, a, b):
        return mm(form, a, b[0]) + mm(form, a, b[1])

    keys_end = (k * end_weight).astype(BF16)
    block_state = mm("htd,hte->hde", keys_end, v)
    prev_state = split(two_level_sum(block_state, decay_rate, float(length), False, (chunk_first, chunks[0])))
    attn = (mm("htd,hsd->hts", q, k) * mask_decay).astype(BF16)
    inside = mm("hts,hse->hte", attn, v)
    attn_out = (inside + inner_weight * mm_split("htd,hde->hte", q, prev_state)).astype(BF16)

    flat_out = jnp.transpose(attn_out, (1, 0, 2)).reshape(length, heads_here * head_size)
    flat_out = reorder(flat_out, order)

    part, part_there = layer_product(flat_out, out_weight)
    from_pair = lax.optimization_barrier((swap(part_there), chunks[1]))[0]

    def partial_rows(start, size):
        rows = slice(start, start + size)
        return part[rows] + from_pair[rows].astype(F32)

    moving = lax.ppermute(partial_rows(96, 16).astype(BF16), "head", COLLECT)
    moved = [moving]
    moving = moving.astype(F32)
    zero = jnp.zeros_like(moving)
    moving = jnp.where(
        core == 0,
        jnp.concatenate([moving, zero], axis=0),
        jnp.concatenate([zero, moving], axis=0),
    )
    for at in (64, 32, 0):
        moving = (moving + partial_rows(at, 32)).astype(BF16)
        moved.append(lax.ppermute(moving, "head", COLLECT))
        moving = moved[-1].astype(F32)
    moving = moved[-1]
    for_here = lax.dynamic_slice_in_dim(moving, core * 16, 16, axis=0)
    for_there = lax.dynamic_slice_in_dim(moving, (1 - core) * 16, 16, axis=0)
    layer_out = partial_rows(112, 16) + for_here.astype(F32) + swap(for_there).astype(F32)
    layer_out = layer_out.astype(BF16)

    packed_there = lax.optimization_barrier((packed_there, moved[0]))[0]
    g = grad_product(order.astype(jnp.int32), packed, packed_there, out_weight)

    cols_here = lax.optimization_barrier((cols_here, g))[0]
    cols_there = swap(cols_here)

    held = [flat_out[:, :256], flat_out[:, 256:]]
    for step in range(3):
        got = [
            lax.ppermute(held[p], ("ctx", "head"), step_pairs(p, step)) for p in range(2)
        ]
        got = list(lax.optimization_barrier((*got, (chunks[2], quarter, g)[step]))[:2])
        held = [jnp.concatenate([held[p], got[p]], axis=0) for p in range(2)]
    last = [lax.ppermute(held[p], ("ctx", "head"), step_pairs(p, 3)) for p in range(2)]

    queries_start = (q * start_weight).astype(BF16)
    grad_block = mm("htd,hte->hde", queries_start, g)
    next_grad = split(two_level_sum(grad_block, decay_rate, float(length), True, moved[2:]))
    grad_scores = (mm("hte,hse->hts", g, v) * mask_decay).astype(BF16)
    query_grad = mm("hts,hsd->htd", grad_scores, k) + inner_weight * mm_split(
        "hte,hde->htd", g, prev_state
    )
    key_grad = mm("hts,htd->hsd", grad_scores, q) + tail_weight * mm_split(
        "hse,hde->hsd", v, next_grad
    )
    value_grad = mm("hts,hte->hse", attn, g) + tail_weight * mm_split(
        "hsd,hde->hse", k, next_grad
    )

    masks = jnp.asarray(
        [[gather_masks(ORDERS[p][c]) for p in range(2)] for c in range(2)], jnp.int32
    )
    table = ctx.astype(jnp.int32) ^ jnp.where(core == 0, masks[0], masks[1])
    weight_grad = weight_product(table[:, :8], held, cols_here, cols_there, None)
    weight_grad = weight_product(table[:, 8:], last, cols_here, cols_there, weight_grad)

    def back(a):
        return jnp.transpose(a, (1, 0, 2)).astype(BF16)

    return (layer_out, back(query_grad), back(key_grad), back(value_grad), weight_grad)


def solution(mesh):
    return jax.shard_map(
        body,
        mesh=mesh,
        in_specs=(
            P("ctx", "head", None),
            P("ctx", "head", None),
            P("ctx", "head", None),
            P("head", None),
            P("head"),
            P(("ctx", "head"), None),
        ),
        out_specs=(
            P(("ctx", "head"), None),
            P("ctx", "head", None),
            P("ctx", "head", None),
            P("ctx", "head", None),
            P("head", "ctx"),
        ),
        check_vma=False,
    )
```

```python
import jax
import jax.numpy as jnp
from jax import lax
from jax.experimental import pallas as pl
from jax.experimental.pallas import tpu as pltpu
from jax.sharding import PartitionSpec as P

F32 = jnp.float32
BF16 = jnp.bfloat16
N_CTX = 16
N_Z = 8

CORE_PAIR = [(h, h ^ 1) for h in range(16)]
SPREAD = [(h, (h - 2 if h % 2 == 0 else h + 2) % 16) for h in range(16)]
COLLECT = [(h, (h + 2 if h % 2 == 0 else h - 2) % 16) for h in range(16)]
ORDERS = (((1, 3, 4, 12), (4, 12, 1, 3)), ((3, 1, 12, 4), (12, 4, 3, 1)))


def x_shift(d):
    return [(c, (c + 4 * d) % 16) for c in range(16)]


def y_shift(d):
    return [(c, (c // 4) * 4 + (c + d) % 4) for c in range(16)]


def step_pairs(pair, step):
    masks = [ORDERS[pair][core][step] for core in range(2)]
    return [
        (c * 16 + h, (c ^ masks[h % 2]) * 16 + h) for c in range(16) for h in range(16)
    ]


def gather_masks(order):
    masks = [0]
    for mask in order:
        masks = masks + [m ^ mask for m in masks]
    return masks


def two_level_sum(state, rate, length, reverse, ties, first=None):
    place = lax.axis_index("ctx")
    x, y = place // 4, place % 4
    sign = -1 if reverse else 1

    def power(n):
        return jnp.exp(-rate * (length * n.astype(F32)))[:, None, None]

    def ahead(at, d):
        return (at >= d) if not reverse else (at + d <= 3)

    def level(own, at, shift, scale, tie, first=None):
        sent = own.astype(BF16)
        if first is not None:
            sent = lax.optimization_barrier((sent, first))[0]
        got = [lax.ppermute(sent, "ctx", shift(sign * d)) for d in (1, 2, 3)]
        if tie is not None:
            got = lax.optimization_barrier((*got, tie))[:3]
        got = [part.astype(F32) for part in got]
        before = 0.0
        for d in (1, 2, 3):
            weight = jnp.where(ahead(at, d), power(jnp.asarray((d - 1) * scale)), 0.0)
            before = before + weight * got[d - 1]
        return before, got

    before_y, got = level(state, y, y_shift, 1, ties[0], first)
    to_end = (3 - y) if not reverse else y
    total = power(to_end) * state
    for d in (1, 2, 3):
        source = (y - sign * d) % 4
        left = (3 - source) if not reverse else source
        total = total + power(left) * got[d - 1]
    tie = ties[1](total) if callable(ties[1]) else ties[1]
    before_x, _ = level(total, x, x_shift, 4, tie)
    steps = y if not reverse else 3 - y
    return before_y + power(steps) * before_x


def weight_kernel(first, table, a0, a1, ours, theirs, *refs):
    out = refs[-1]
    for pair, part in enumerate((a0, a1)):
        rows = slice(pair * 256, (pair + 1) * 256)
        total = jnp.zeros((256, 384), F32) if first else refs[0][rows, :]
        for i in range(8):
            at = table[pair, i]
            block = jnp.concatenate([ours[at], theirs[at]], axis=0)
            total = total + lax.dot_general(
                part[i * 256 : (i + 1) * 256, :],
                block,
                (((0,), (0,)), ((), ())),
                preferred_element_type=F32,
            )
        out[rows, :] = total


def weight_product(table, parts, ours, theirs, earlier):
    first = earlier is None
    operands = list(parts) + [ours, theirs] + ([] if first else [earlier])
    return pl.pallas_call(
        lambda *refs: weight_kernel(first, *refs),
        out_shape=jax.ShapeDtypeStruct((512, 384), F32),
        in_specs=[pl.BlockSpec(memory_space=pltpu.SMEM)]
        + [pl.BlockSpec(memory_space=pltpu.VMEM)] * len(operands),
        out_specs=pl.BlockSpec(memory_space=pltpu.VMEM),
        compiler_params=pltpu.CompilerParams(vmem_limit_bytes=32 * 2**20),
        cost_estimate=pl.CostEstimate(
            flops=2 * 2048 * 512 * 384, bytes_accessed=6 * 2**20, transcendentals=0
        ),
    )(table, *operands)


def pack_kernel(c1, c2, c3, quarter, own, out):
    n_col = out.shape[2]
    row = 0
    for part in (c1, c2, c3, quarter, own):
        size = part.shape[0]
        for c in range(out.shape[0]):
            out[c, row : row + size, :] = part[:, c * n_col : (c + 1) * n_col]
        row += size


def pack_columns(parts, n_col):
    return pl.pallas_call(
        pack_kernel,
        out_shape=jax.ShapeDtypeStruct((N_CTX, 128, n_col), BF16),
        in_specs=[pl.BlockSpec(memory_space=pltpu.VMEM)] * 5,
        out_specs=pl.BlockSpec(memory_space=pltpu.VMEM),
        compiler_params=pltpu.CompilerParams(vmem_limit_bytes=16 * 2**20),
        cost_estimate=pl.CostEstimate(flops=0, bytes_accessed=3 * 2**20, transcendentals=0),
    )(*parts)


def grad_kernel(order, ours, theirs, weight, out, total):
    step = pl.program_id(0)

    @pl.when(step == 0)
    def _():
        total[...] = jnp.zeros_like(total)

    n_col = ours.shape[2]
    for c in range(ours.shape[0]):
        total[...] += lax.dot_general(
            jnp.concatenate([ours[c], theirs[c]], axis=0),
            weight[:, c * n_col : (c + 1) * n_col],
            (((1,), (1,)), ((), ())),
            preferred_element_type=F32,
        )

    @pl.when(step == pl.num_programs(0) - 1)
    def _():
        for piece in range(16):
            to = pl.ds(pl.multiple_of(order[piece] * 16, 16), 16)
            rows = total[piece * 16 : (piece + 1) * 16, :].astype(BF16)
            for j in range(4):
                out[j, to, :] = rows[:, j * 128 : (j + 1) * 128]


def grad_product(order, ours, theirs, weight):
    n_col = ours.shape[2]
    rows_spec = pl.BlockSpec((4, 128, n_col), lambda i: (i, 0, 0))
    return pl.pallas_call(
        grad_kernel,
        out_shape=jax.ShapeDtypeStruct((4, 256, 128), BF16),
        grid=(4,),
        in_specs=[pl.BlockSpec(memory_space=pltpu.SMEM), rows_spec, rows_spec, pl.BlockSpec((512, 4 * n_col), lambda i: (0, i))],
        out_specs=pl.BlockSpec((4, 256, 128), lambda i: (0, 0, 0)),
        scratch_shapes=[pltpu.VMEM((256, 512), F32)],
        compiler_params=pltpu.CompilerParams(vmem_limit_bytes=58 * 2**20),
        cost_estimate=pl.CostEstimate(
            flops=2 * 256 * 512 * 6144, bytes_accessed=10 * 2**20, transcendentals=0
        ),
    )(order, ours, theirs, weight)


def layer_kernel(flat, weight, ours, theirs):
    both = jnp.dot(flat[...], weight[...], preferred_element_type=F32)
    ours[...] = both[:128]
    theirs[...] = both[128:].astype(BF16)


def layer_product(flat, weight):
    width = weight.shape[1] // 4
    return pl.pallas_call(
        layer_kernel,
        out_shape=(
            jax.ShapeDtypeStruct((128, 4 * width), F32),
            jax.ShapeDtypeStruct((128, 4 * width), BF16),
        ),
        grid=(4,),
        in_specs=[
            pl.BlockSpec((256, 512), lambda i: (0, 0)),
            pl.BlockSpec((512, width), lambda i: (0, i)),
        ],
        out_specs=(
            pl.BlockSpec((128, width), lambda i: (0, i)),
            pl.BlockSpec((128, width), lambda i: (0, i)),
        ),
        compiler_params=pltpu.CompilerParams(vmem_limit_bytes=58 * 2**20),
        cost_estimate=pl.CostEstimate(
            flops=2 * 256 * 512 * 6144, bytes_accessed=11 * 2**20, transcendentals=0
        ),
    )(flat, weight)


def body(queries, keys, values, out_weight, decay_rate, out_grad):
    length, heads_here, head_size = queries.shape
    ctx = lax.axis_index("ctx")
    head = lax.axis_index("head")
    z, core = head // 2, head % 2
    n_col = out_grad.shape[1] // N_CTX

    sign = 1 - 2 * core

    def swap(a):
        return lax.ppermute(a, "head", CORE_PAIR)

    def half_order(of_core, s):
        pieces = []
        for k in (1, 2, 3):
            base = 2 * ((z + s * k) % 8)
            pieces += [base, base + 1]
        return pieces + [2 * ((z + 4) % 8) + of_core, 2 * z + of_core]

    order = jnp.stack(half_order(core, sign) + half_order(1 - core, -sign))
    def reorder(a, by):
        return jnp.take(a.reshape(16, 16, -1), by, axis=0, mode="clip").reshape(a.shape)

    other = swap(out_grad)
    chunk = jnp.where(
        core == 0,
        jnp.concatenate([out_grad, other], axis=0),
        jnp.concatenate([other, out_grad], axis=0),
    )
    chunk_first = chunk
    chunks = []
    for k in (1, 2, 3):
        chunk = lax.ppermute(chunk, "head", SPREAD)
        chunks.append(chunk)
    places = jnp.arange(length, dtype=F32)
    offsets = places[:, None] - places[None, :]
    mask_decay = jnp.where(
        offsets[None] >= 0,
        jnp.exp(-decay_rate[:, None, None] * jnp.maximum(offsets, 0.0)[None]),
        0.0,
    )

    def decay(n):
        return jnp.exp(-decay_rate[:, None] * n[None, :])[:, :, None]

    end_weight = decay(length - 1.0 - places)
    start_weight = decay(places)
    inner_weight = decay(places + 1.0)
    tail_weight = decay(length - places)

    q = jnp.transpose(queries, (1, 0, 2))
    k = jnp.transpose(keys, (1, 0, 2))
    v = jnp.transpose(values, (1, 0, 2))

    def mm(form, a, b):
        return jnp.einsum(form, a, b, preferred_element_type=F32)

    def split(a):
        high = a.astype(BF16)
        return high, (a - high.astype(F32)).astype(BF16)

    def mm_split(form, a, b):
        return mm(form, a, b[0]) + mm(form, a, b[1])

    keys_end = (k * end_weight).astype(BF16)
    block_state = mm("htd,hte->hde", keys_end, v)
    prev_state = split(two_level_sum(block_state, decay_rate, float(length), False, (chunk_first, chunks[0])))
    attn = (mm("htd,hsd->hts", q, k) * mask_decay).astype(BF16)
    inside = mm("hts,hse->hte", attn, v)
    attn_out = (inside + inner_weight * mm_split("htd,hde->hte", q, prev_state)).astype(BF16)

    flat_out = jnp.transpose(attn_out, (1, 0, 2)).reshape(length, heads_here * head_size)
    flat_out = reorder(flat_out, order)

    def gather_step(held, step):
        return [
            lax.ppermute(held[p], ("ctx", "head"), step_pairs(p, step)) for p in range(2)
        ]

    def joined(held, got):
        return [jnp.concatenate([held[p], got[p]], axis=0) for p in range(2)]

    def after(a, other):
        return lax.optimization_barrier((a, other))[0]

    held = [flat_out[:, :256], flat_out[:, 256:]]
    got = gather_step(held, 0)
    part, part_there = layer_product(after(flat_out, chunks[1]), out_weight)
    from_pair = swap(after(part_there, got))
    held = joined(held, got)
    got = gather_step(held, 1)
    chunk = after(chunk, got)
    quarter = lax.dynamic_slice_in_dim(chunk, core * 16, 16, axis=0)
    quarter = lax.ppermute(quarter, "head", SPREAD)
    held = joined(held, got)
    got = gather_step(held, 2)

    def partial_rows(start, size):
        rows = slice(start, start + size)
        return part[rows] + from_pair[rows].astype(F32)

    moving = lax.ppermute(partial_rows(96, 16).astype(BF16), "head", COLLECT)
    moved = [moving]
    moving = moving.astype(F32)

    packed = pack_columns((*chunks, after(quarter, (got, moved[0])), out_grad), n_col)
    packed_there = swap(packed)
    cols_here = lax.all_to_all(packed, "ctx", split_axis=0, concat_axis=0, tiled=True)
    held = joined(held, got)
    last = gather_step(held, 3)

    moving = after(moving, packed)
    zero = jnp.zeros_like(moving)
    moving = jnp.where(
        core == 0,
        jnp.concatenate([moving, zero], axis=0),
        jnp.concatenate([zero, moving], axis=0),
    )
    for at in (64, 32, 0):
        moving = (moving + partial_rows(at, 32)).astype(BF16)
        moved.append(lax.ppermute(moving, "head", COLLECT))
        moving = moved[-1].astype(F32)
    moving = moved[-1]
    for_here = lax.dynamic_slice_in_dim(moving, core * 16, 16, axis=0)
    for_there = lax.dynamic_slice_in_dim(moving, (1 - core) * 16, 16, axis=0)
    layer_out = partial_rows(112, 16) + for_here.astype(F32) + swap(for_there).astype(F32)
    layer_out = layer_out.astype(BF16)

    packed_there = after(packed_there, moved[0])
    g = grad_product(order.astype(jnp.int32), packed, packed_there, out_weight)

    masks = jnp.asarray(
        [[gather_masks(ORDERS[p][c]) for p in range(2)] for c in range(2)], jnp.int32
    )
    table = ctx.astype(jnp.int32) ^ jnp.where(core == 0, masks[0], masks[1])

    def weights(before):
        ours = after(cols_here, before)
        theirs = swap(ours)
        first = weight_product(table[:, :8], held, ours, theirs, None)
        return weight_product(table[:, 8:], last, ours, theirs, first)

    finished = []

    def while_last_level(total):
        finished.append(weights(total))
        return moved[3], finished[0]

    queries_start = (q * start_weight).astype(BF16)
    grad_block = mm("htd,hte->hde", queries_start, g)
    next_grad = split(
        two_level_sum(
            grad_block, decay_rate, float(length), True, (moved[2], while_last_level), (last, moved[1])
        )
    )
    weight_grad = finished[0]
    grad_scores = (mm("hte,hse->hts", g, v) * mask_decay).astype(BF16)
    query_grad = mm("hts,hsd->htd", grad_scores, k) + inner_weight * mm_split(
        "hte,hde->htd", g, prev_state
    )
    key_grad = mm("hts,htd->hsd", grad_scores, q) + tail_weight * mm_split(
        "hse,hde->hsd", v, next_grad
    )
    value_grad = mm("hts,hte->hse", attn, g) + tail_weight * mm_split(
        "hsd,hde->hse", k, next_grad
    )

    def back(a):
        return jnp.transpose(a, (1, 0, 2)).astype(BF16)

    return (layer_out, back(query_grad), back(key_grad), back(value_grad), weight_grad)


def solution(mesh):
    return jax.shard_map(
        body,
        mesh=mesh,
        in_specs=(
            P("ctx", "head", None),
            P("ctx", "head", None),
            P("ctx", "head", None),
            P("head", None),
            P("head"),
            P(("ctx", "head"), None),
        ),
        out_specs=(
            P(("ctx", "head"), None),
            P("ctx", "head", None),
            P("ctx", "head", None),
            P("ctx", "head", None),
            P("head", "ctx"),
        ),
        check_vma=False,
    )
```

```python
import jax
import jax.numpy as jnp
from jax import lax
from jax.experimental import pallas as pl
from jax.experimental.pallas import tpu as pltpu
from jax.sharding import PartitionSpec as P

F32 = jnp.float32
BF16 = jnp.bfloat16
N_CTX = 16
N_Z = 8

CORE_PAIR = [(h, h ^ 1) for h in range(16)]
SPREAD = [(h, (h - 2 if h % 2 == 0 else h + 2) % 16) for h in range(16)]
COLLECT = [(h, (h + 2 if h % 2 == 0 else h - 2) % 16) for h in range(16)]
ORDERS = (((1, 3, 4, 12), (4, 12, 1, 3)), ((3, 1, 12, 4), (12, 4, 3, 1)))


def x_shift(d):
    return [(c, (c + 4 * d) % 16) for c in range(16)]


def y_shift(d):
    return [(c, (c // 4) * 4 + (c + d) % 4) for c in range(16)]


def step_pairs(pair, step):
    masks = [ORDERS[pair][core][step] for core in range(2)]
    return [
        (c * 16 + h, (c ^ masks[h % 2]) * 16 + h) for c in range(16) for h in range(16)
    ]


def gather_masks(order):
    masks = [0]
    for mask in order:
        masks = masks + [m ^ mask for m in masks]
    return masks


def two_level_sum(state, rate, length, reverse, ties, first=None):
    place = lax.axis_index("ctx")
    x, y = place // 4, place % 4
    sign = -1 if reverse else 1

    def power(n):
        return jnp.exp(-rate * (length * n.astype(F32)))[:, None, None]

    def ahead(at, d):
        return (at >= d) if not reverse else (at + d <= 3)

    def level(own, at, shift, scale, tie, first=None):
        sent = own.astype(BF16)
        if first is not None:
            sent = lax.optimization_barrier((sent, first))[0]
        got = [lax.ppermute(sent, "ctx", shift(sign * d)) for d in (1, 2, 3)]
        if tie is not None:
            got = lax.optimization_barrier((*got, tie))[:3]
        got = [part.astype(F32) for part in got]
        before = 0.0
        for d in (1, 2, 3):
            weight = jnp.where(ahead(at, d), power(jnp.asarray((d - 1) * scale)), 0.0)
            before = before + weight * got[d - 1]
        return before, got

    before_y, got = level(state, y, y_shift, 1, ties[0], first)
    to_end = (3 - y) if not reverse else y
    total = power(to_end) * state
    for d in (1, 2, 3):
        source = (y - sign * d) % 4
        left = (3 - source) if not reverse else source
        total = total + power(left) * got[d - 1]
    tie = ties[1](total) if callable(ties[1]) else ties[1]
    before_x, _ = level(total, x, x_shift, 4, tie)
    steps = y if not reverse else 3 - y
    return before_y + power(steps) * before_x


def weight_kernel(first, table, a0, a1, ours, theirs, *refs):
    out = refs[-1]
    for pair, part in enumerate((a0, a1)):
        rows = slice(pair * 256, (pair + 1) * 256)
        total = jnp.zeros((256, 384), F32) if first else refs[0][rows, :]
        for i in range(8):
            at = table[pair, i]
            block = jnp.concatenate([ours[at], theirs[at]], axis=0)
            total = total + lax.dot_general(
                part[i * 256 : (i + 1) * 256, :],
                block,
                (((0,), (0,)), ((), ())),
                preferred_element_type=F32,
            )
        out[rows, :] = total


def weight_product(table, parts, ours, theirs, earlier):
    first = earlier is None
    operands = list(parts) + [ours, theirs] + ([] if first else [earlier])
    return pl.pallas_call(
        lambda *refs: weight_kernel(first, *refs),
        out_shape=jax.ShapeDtypeStruct((512, 384), F32),
        in_specs=[pl.BlockSpec(memory_space=pltpu.SMEM)]
        + [pl.BlockSpec(memory_space=pltpu.VMEM)] * len(operands),
        out_specs=pl.BlockSpec(memory_space=pltpu.VMEM),
        compiler_params=pltpu.CompilerParams(vmem_limit_bytes=32 * 2**20),
        cost_estimate=pl.CostEstimate(
            flops=2 * 2048 * 512 * 384, bytes_accessed=6 * 2**20, transcendentals=0
        ),
    )(table, *operands)


def pack_kernel(c1, c2, c3, quarter, own, out):
    n_col = out.shape[2]
    row = 0
    for part in (c1, c2, c3, quarter, own):
        size = part.shape[0]
        for c in range(out.shape[0]):
            out[c, row : row + size, :] = part[:, c * n_col : (c + 1) * n_col]
        row += size


def pack_columns(parts, n_col):
    return pl.pallas_call(
        pack_kernel,
        out_shape=jax.ShapeDtypeStruct((N_CTX, 128, n_col), BF16),
        in_specs=[pl.BlockSpec(memory_space=pltpu.VMEM)] * 5,
        out_specs=pl.BlockSpec(memory_space=pltpu.VMEM),
        compiler_params=pltpu.CompilerParams(vmem_limit_bytes=16 * 2**20),
        cost_estimate=pl.CostEstimate(flops=0, bytes_accessed=3 * 2**20, transcendentals=0),
    )(*parts)


def grad_kernel(order, ours, theirs, weight, out, total):
    step = pl.program_id(0)

    @pl.when(step == 0)
    def _():
        total[...] = jnp.zeros_like(total)

    n_col = ours.shape[2]
    for c in range(ours.shape[0]):
        total[...] += lax.dot_general(
            jnp.concatenate([ours[c], theirs[c]], axis=0),
            weight[:, c * n_col : (c + 1) * n_col],
            (((1,), (1,)), ((), ())),
            preferred_element_type=F32,
        )

    @pl.when(step == pl.num_programs(0) - 1)
    def _():
        for piece in range(16):
            to = pl.ds(pl.multiple_of(order[piece] * 16, 16), 16)
            rows = total[piece * 16 : (piece + 1) * 16, :].astype(BF16)
            for j in range(4):
                out[j, to, :] = rows[:, j * 128 : (j + 1) * 128]


def grad_product(order, ours, theirs, weight):
    n_col = ours.shape[2]
    rows_spec = pl.BlockSpec((4, 128, n_col), lambda i: (i, 0, 0))
    return pl.pallas_call(
        grad_kernel,
        out_shape=jax.ShapeDtypeStruct((4, 256, 128), BF16),
        grid=(4,),
        in_specs=[pl.BlockSpec(memory_space=pltpu.SMEM), rows_spec, rows_spec, pl.BlockSpec((512, 4 * n_col), lambda i: (0, i))],
        out_specs=pl.BlockSpec((4, 256, 128), lambda i: (0, 0, 0)),
        scratch_shapes=[pltpu.VMEM((256, 512), F32)],
        compiler_params=pltpu.CompilerParams(vmem_limit_bytes=58 * 2**20),
        cost_estimate=pl.CostEstimate(
            flops=2 * 256 * 512 * 6144, bytes_accessed=10 * 2**20, transcendentals=0
        ),
    )(order, ours, theirs, weight)


def layer_kernel(flat, weight, ours, theirs):
    both = jnp.dot(flat[...], weight[...], preferred_element_type=F32)
    ours[...] = both[:128]
    theirs[...] = both[128:].astype(BF16)


def layer_product(flat, weight):
    width = weight.shape[1] // 4
    return pl.pallas_call(
        layer_kernel,
        out_shape=(
            jax.ShapeDtypeStruct((128, 4 * width), F32),
            jax.ShapeDtypeStruct((128, 4 * width), BF16),
        ),
        grid=(4,),
        in_specs=[
            pl.BlockSpec((256, 512), lambda i: (0, 0)),
            pl.BlockSpec((512, width), lambda i: (0, i)),
        ],
        out_specs=(
            pl.BlockSpec((128, width), lambda i: (0, i)),
            pl.BlockSpec((128, width), lambda i: (0, i)),
        ),
        compiler_params=pltpu.CompilerParams(vmem_limit_bytes=58 * 2**20),
        cost_estimate=pl.CostEstimate(
            flops=2 * 256 * 512 * 6144, bytes_accessed=11 * 2**20, transcendentals=0
        ),
    )(flat, weight)


def body(queries, keys, values, out_weight, decay_rate, out_grad):
    length, heads_here, head_size = queries.shape
    ctx = lax.axis_index("ctx")
    head = lax.axis_index("head")
    z, core = head // 2, head % 2
    n_col = out_grad.shape[1] // N_CTX

    sign = 1 - 2 * core

    def swap(a):
        return lax.ppermute(a, "head", CORE_PAIR)

    def half_order(of_core, s):
        pieces = []
        for k in (1, 2, 3):
            base = 2 * ((z + s * k) % 8)
            pieces += [base, base + 1]
        return pieces + [2 * ((z + 4) % 8) + of_core, 2 * z + of_core]

    order = jnp.stack(half_order(core, sign) + half_order(1 - core, -sign))
    def reorder(a, by):
        return jnp.take(a.reshape(16, 16, -1), by, axis=0, mode="clip").reshape(a.shape)

    other = swap(out_grad)
    chunk = jnp.where(
        core == 0,
        jnp.concatenate([out_grad, other], axis=0),
        jnp.concatenate([other, out_grad], axis=0),
    )
    chunk_first = chunk
    chunks = []
    for k in (1, 2, 3):
        chunk = lax.ppermute(chunk, "head", SPREAD)
        chunks.append(chunk)
    places = jnp.arange(length, dtype=F32)
    offsets = places[:, None] - places[None, :]
    mask_decay = jnp.where(
        offsets[None] >= 0,
        jnp.exp(-decay_rate[:, None, None] * jnp.maximum(offsets, 0.0)[None]),
        0.0,
    )

    def decay(n):
        return jnp.exp(-decay_rate[:, None] * n[None, :])[:, :, None]

    end_weight = decay(length - 1.0 - places)
    start_weight = decay(places)
    inner_weight = decay(places + 1.0)
    tail_weight = decay(length - places)

    q = jnp.transpose(queries, (1, 0, 2))
    k = jnp.transpose(keys, (1, 0, 2))
    v = jnp.transpose(values, (1, 0, 2))

    def mm(form, a, b):
        return jnp.einsum(form, a, b, preferred_element_type=F32)

    def split(a):
        high = a.astype(BF16)
        return high, (a - high.astype(F32)).astype(BF16)

    def mm_split(form, a, b):
        return mm(form, a, b[0]) + mm(form, a, b[1])

    keys_end = (k * end_weight).astype(BF16)
    block_state = mm("htd,hte->hde", keys_end, v)
    prev_state = split(two_level_sum(block_state, decay_rate, float(length), False, (chunk_first, chunks[0])))
    attn = (mm("htd,hsd->hts", q, k) * mask_decay).astype(BF16)
    inside = mm("hts,hse->hte", attn, v)
    attn_out = (inside + inner_weight * mm_split("htd,hde->hte", q, prev_state)).astype(BF16)

    flat_out = jnp.transpose(attn_out, (1, 0, 2)).reshape(length, heads_here * head_size)
    flat_out = reorder(flat_out, order)

    def gather_step(held, step):
        return [
            lax.ppermute(held[p], ("ctx", "head"), step_pairs(p, step)) for p in range(2)
        ]

    def joined(held, got):
        return [jnp.concatenate([held[p], got[p]], axis=0) for p in range(2)]

    def after(a, other):
        return lax.optimization_barrier((a, other))[0]

    held = [flat_out[:, :256], flat_out[:, 256:]]
    got = gather_step(held, 0)
    part, part_there = layer_product(after(flat_out, chunks[1]), out_weight)
    from_pair = swap(after(part_there, got))
    held = joined(held, got)
    got = gather_step(held, 1)
    chunk = after(chunk, got)
    quarter = lax.dynamic_slice_in_dim(chunk, core * 16, 16, axis=0)
    quarter = lax.ppermute(quarter, "head", SPREAD)
    held = joined(held, got)
    got = gather_step(held, 2)

    packed = pack_columns((*chunks, after(quarter, got), out_grad), n_col)
    packed_there = swap(packed)
    cols_here = lax.all_to_all(packed, "ctx", split_axis=0, concat_axis=0, tiled=True)
    held = joined(held, got)
    last = gather_step(held, 3)

    def partial_rows(start, size):
        rows = slice(start, start + size)
        return part[rows] + from_pair[rows].astype(F32)

    moving = lax.ppermute(partial_rows(96, 16).astype(BF16), "head", COLLECT)
    moved = [moving]
    moving = moving.astype(F32)
    zero = jnp.zeros_like(moving)
    moving = jnp.where(
        core == 0,
        jnp.concatenate([moving, zero], axis=0),
        jnp.concatenate([zero, moving], axis=0),
    )
    for at in (64, 32):
        moving = (moving + partial_rows(at, 32)).astype(BF16)
        moved.append(lax.ppermute(moving, "head", COLLECT))
        moving = moved[-1].astype(F32)

    packed_there = lax.optimization_barrier((packed_there, moved[0]))[0]
    g = grad_product(order.astype(jnp.int32), packed, packed_there, out_weight)

    masks = jnp.asarray(
        [[gather_masks(ORDERS[p][c]) for p in range(2)] for c in range(2)], jnp.int32
    )
    table = ctx.astype(jnp.int32) ^ jnp.where(core == 0, masks[0], masks[1])

    def weights(before):
        ours = after(cols_here, before)
        theirs = swap(ours)
        first = weight_product(table[:, :8], held, ours, theirs, None)
        return weight_product(table[:, 8:], last, ours, theirs, first)

    finished = []

    def while_last_level(total):
        finished.append(weights(total))
        chunk = after((moving + partial_rows(0, 32)).astype(BF16), total)
        finished.append(lax.ppermute(chunk, "head", COLLECT))
        return finished[0]

    queries_start = (q * start_weight).astype(BF16)
    grad_block = mm("htd,hte->hde", queries_start, g)
    next_grad = split(
        two_level_sum(
            grad_block, decay_rate, float(length), True, (moved[2], while_last_level), last
        )
    )
    weight_grad = finished[0]
    moving = after(finished[1], next_grad[0])
    for_here = lax.dynamic_slice_in_dim(moving, core * 16, 16, axis=0)
    for_there = lax.dynamic_slice_in_dim(moving, (1 - core) * 16, 16, axis=0)
    layer_out = partial_rows(112, 16) + for_here.astype(F32) + swap(for_there).astype(F32)
    layer_out = layer_out.astype(BF16)

    grad_scores = (mm("hte,hse->hts", g, v) * mask_decay).astype(BF16)
    query_grad = mm("hts,hsd->htd", grad_scores, k) + inner_weight * mm_split(
        "hte,hde->htd", g, prev_state
    )
    key_grad = mm("hts,htd->hsd", grad_scores, q) + tail_weight * mm_split(
        "hse,hde->hsd", v, next_grad
    )
    value_grad = mm("hts,hte->hse", attn, g) + tail_weight * mm_split(
        "hsd,hde->hse", k, next_grad
    )

    def back(a):
        return jnp.transpose(a, (1, 0, 2)).astype(BF16)

    return (layer_out, back(query_grad), back(key_grad), back(value_grad), weight_grad)


def solution(mesh):
    return jax.shard_map(
        body,
        mesh=mesh,
        in_specs=(
            P("ctx", "head", None),
            P("ctx", "head", None),
            P("ctx", "head", None),
            P("head", None),
            P("head"),
            P(("ctx", "head"), None),
        ),
        out_specs=(
            P(("ctx", "head"), None),
            P("ctx", "head", None),
            P("ctx", "head", None),
            P("ctx", "head", None),
            P("head", "ctx"),
        ),
        check_vma=False,
    )
```

```python
import jax
import jax.numpy as jnp
from jax import lax
from jax.experimental import pallas as pl
from jax.experimental.pallas import tpu as pltpu
from jax.sharding import PartitionSpec as P

F32 = jnp.float32
BF16 = jnp.bfloat16
N_CTX = 16
N_Z = 8

CORE_PAIR = [(h, h ^ 1) for h in range(16)]
SPREAD = [(h, (h - 2 if h % 2 == 0 else h + 2) % 16) for h in range(16)]
COLLECT = [(h, (h + 2 if h % 2 == 0 else h - 2) % 16) for h in range(16)]
ORDERS = (((1, 3, 4, 12), (4, 12, 1, 3)), ((3, 1, 12, 4), (12, 4, 3, 1)))


def x_shift(d):
    return [(c, (c + 4 * d) % 16) for c in range(16)]


def y_shift(d):
    return [(c, (c // 4) * 4 + (c + d) % 4) for c in range(16)]


def step_pairs(pair, step):
    masks = [ORDERS[pair][core][step] for core in range(2)]
    return [
        (c * 16 + h, (c ^ masks[h % 2]) * 16 + h) for c in range(16) for h in range(16)
    ]


def gather_masks(order):
    masks = [0]
    for mask in order:
        masks = masks + [m ^ mask for m in masks]
    return masks


def two_level_sum(state, rate, length, reverse, ties, first=None):
    place = lax.axis_index("ctx")
    x, y = place // 4, place % 4
    sign = -1 if reverse else 1

    def power(n):
        return jnp.exp(-rate * (length * n.astype(F32)))[:, None, None]

    def ahead(at, d):
        return (at >= d) if not reverse else (at + d <= 3)

    def level(own, at, shift, scale, tie, first=None):
        sent = own.astype(BF16)
        if first is not None:
            sent = lax.optimization_barrier((sent, first))[0]
        got = [lax.ppermute(sent, "ctx", shift(sign * d)) for d in (1, 2, 3)]
        if tie is not None:
            got = lax.optimization_barrier((*got, tie))[:3]
        got = [part.astype(F32) for part in got]
        before = 0.0
        for d in (1, 2, 3):
            weight = jnp.where(ahead(at, d), power(jnp.asarray((d - 1) * scale)), 0.0)
            before = before + weight * got[d - 1]
        return before, got

    before_y, got = level(state, y, y_shift, 1, ties[0], first)
    to_end = (3 - y) if not reverse else y
    total = power(to_end) * state
    for d in (1, 2, 3):
        source = (y - sign * d) % 4
        left = (3 - source) if not reverse else source
        total = total + power(left) * got[d - 1]
    tie = ties[1](total) if callable(ties[1]) else ties[1]
    before_x, _ = level(total, x, x_shift, 4, tie)
    steps = y if not reverse else 3 - y
    return before_y + power(steps) * before_x


def weight_kernel(first, table, a0, a1, ours, theirs, *refs):
    out = refs[-1]
    for pair, part in enumerate((a0, a1)):
        rows = slice(pair * 256, (pair + 1) * 256)
        total = jnp.zeros((256, 384), F32) if first else refs[0][rows, :]
        for i in range(8):
            at = table[pair, i]
            block = jnp.concatenate([ours[at], theirs[at]], axis=0)
            total = total + lax.dot_general(
                part[i * 256 : (i + 1) * 256, :],
                block,
                (((0,), (0,)), ((), ())),
                preferred_element_type=F32,
            )
        out[rows, :] = total


def weight_product(table, parts, ours, theirs, earlier):
    first = earlier is None
    operands = list(parts) + [ours, theirs] + ([] if first else [earlier])
    return pl.pallas_call(
        lambda *refs: weight_kernel(first, *refs),
        out_shape=jax.ShapeDtypeStruct((512, 384), F32),
        in_specs=[pl.BlockSpec(memory_space=pltpu.SMEM)]
        + [pl.BlockSpec(memory_space=pltpu.VMEM)] * len(operands),
        out_specs=pl.BlockSpec(memory_space=pltpu.VMEM),
        compiler_params=pltpu.CompilerParams(vmem_limit_bytes=32 * 2**20),
        cost_estimate=pl.CostEstimate(
            flops=2 * 2048 * 512 * 384, bytes_accessed=6 * 2**20, transcendentals=0
        ),
    )(table, *operands)


def pack_kernel(c1, c2, c3, quarter, own, out):
    n_col = out.shape[2]
    row = 0
    for part in (c1, c2, c3, quarter, own):
        size = part.shape[0]
        for c in range(out.shape[0]):
            out[c, row : row + size, :] = part[:, c * n_col : (c + 1) * n_col]
        row += size


def pack_columns(parts, n_col):
    return pl.pallas_call(
        pack_kernel,
        out_shape=jax.ShapeDtypeStruct((N_CTX, 128, n_col), BF16),
        in_specs=[pl.BlockSpec(memory_space=pltpu.VMEM)] * 5,
        out_specs=pl.BlockSpec(memory_space=pltpu.VMEM),
        compiler_params=pltpu.CompilerParams(vmem_limit_bytes=16 * 2**20),
        cost_estimate=pl.CostEstimate(flops=0, bytes_accessed=3 * 2**20, transcendentals=0),
    )(*parts)


def grad_kernel(order, ours, theirs, weight, out, total):
    step = pl.program_id(0)

    @pl.when(step == 0)
    def _():
        total[...] = jnp.zeros_like(total)

    n_col = ours.shape[2]
    for c in range(ours.shape[0]):
        total[...] += lax.dot_general(
            jnp.concatenate([ours[c], theirs[c]], axis=0),
            weight[:, c * n_col : (c + 1) * n_col],
            (((1,), (1,)), ((), ())),
            preferred_element_type=F32,
        )

    @pl.when(step == pl.num_programs(0) - 1)
    def _():
        for piece in range(16):
            to = pl.ds(pl.multiple_of(order[piece] * 16, 16), 16)
            rows = total[piece * 16 : (piece + 1) * 16, :].astype(BF16)
            for j in range(4):
                out[j, to, :] = rows[:, j * 128 : (j + 1) * 128]


def grad_product(order, ours, theirs, weight):
    n_col = ours.shape[2]
    rows_spec = pl.BlockSpec((4, 128, n_col), lambda i: (i, 0, 0))
    return pl.pallas_call(
        grad_kernel,
        out_shape=jax.ShapeDtypeStruct((4, 256, 128), BF16),
        grid=(4,),
        in_specs=[pl.BlockSpec(memory_space=pltpu.SMEM), rows_spec, rows_spec, pl.BlockSpec((512, 4 * n_col), lambda i: (0, i))],
        out_specs=pl.BlockSpec((4, 256, 128), lambda i: (0, 0, 0)),
        scratch_shapes=[pltpu.VMEM((256, 512), F32)],
        compiler_params=pltpu.CompilerParams(vmem_limit_bytes=58 * 2**20),
        cost_estimate=pl.CostEstimate(
            flops=2 * 256 * 512 * 6144, bytes_accessed=10 * 2**20, transcendentals=0
        ),
    )(order, ours, theirs, weight)


def layer_kernel(flat, weight, ours, theirs):
    both = jnp.dot(flat[...], weight[...], preferred_element_type=F32)
    ours[...] = both[:128]
    theirs[...] = both[128:].astype(BF16)


def layer_product(flat, weight):
    width = weight.shape[1] // 4
    return pl.pallas_call(
        layer_kernel,
        out_shape=(
            jax.ShapeDtypeStruct((128, 4 * width), F32),
            jax.ShapeDtypeStruct((128, 4 * width), BF16),
        ),
        grid=(4,),
        in_specs=[
            pl.BlockSpec((256, 512), lambda i: (0, 0)),
            pl.BlockSpec((512, width), lambda i: (0, i)),
        ],
        out_specs=(
            pl.BlockSpec((128, width), lambda i: (0, i)),
            pl.BlockSpec((128, width), lambda i: (0, i)),
        ),
        compiler_params=pltpu.CompilerParams(vmem_limit_bytes=58 * 2**20),
        cost_estimate=pl.CostEstimate(
            flops=2 * 256 * 512 * 6144, bytes_accessed=11 * 2**20, transcendentals=0
        ),
    )(flat, weight)


def body(queries, keys, values, out_weight, decay_rate, out_grad):
    length, heads_here, head_size = queries.shape
    ctx = lax.axis_index("ctx")
    head = lax.axis_index("head")
    z, core = head // 2, head % 2
    n_col = out_grad.shape[1] // N_CTX

    sign = 1 - 2 * core

    def swap(a):
        return lax.ppermute(a, "head", CORE_PAIR)

    def half_order(of_core, s):
        pieces = []
        for k in (1, 2, 3):
            base = 2 * ((z + s * k) % 8)
            pieces += [base, base + 1]
        return pieces + [2 * ((z + 4) % 8) + of_core, 2 * z + of_core]

    order = jnp.stack(half_order(core, sign) + half_order(1 - core, -sign))
    def reorder(a, by):
        return jnp.take(a.reshape(16, 16, -1), by, axis=0, mode="clip").reshape(a.shape)

    other = swap(out_grad)
    chunk = jnp.where(
        core == 0,
        jnp.concatenate([out_grad, other], axis=0),
        jnp.concatenate([other, out_grad], axis=0),
    )
    chunk_first = chunk
    chunks = []
    for k in (1, 2, 3):
        chunk = lax.ppermute(chunk, "head", SPREAD)
        chunks.append(chunk)
    places = jnp.arange(length, dtype=F32)
    offsets = places[:, None] - places[None, :]
    mask_decay = jnp.where(
        offsets[None] >= 0,
        jnp.exp(-decay_rate[:, None, None] * jnp.maximum(offsets, 0.0)[None]),
        0.0,
    )

    def decay(n):
        return jnp.exp(-decay_rate[:, None] * n[None, :])[:, :, None]

    end_weight = decay(length - 1.0 - places)
    start_weight = decay(places)
    inner_weight = decay(places + 1.0)
    tail_weight = decay(length - places)

    q = jnp.transpose(queries, (1, 0, 2))
    k = jnp.transpose(keys, (1, 0, 2))
    v = jnp.transpose(values, (1, 0, 2))

    def mm(form, a, b):
        return jnp.einsum(form, a, b, preferred_element_type=F32)

    def split(a):
        high = a.astype(BF16)
        return high, (a - high.astype(F32)).astype(BF16)

    def mm_split(form, a, b):
        return mm(form, a, b[0]) + mm(form, a, b[1])

    keys_end = (k * end_weight).astype(BF16)
    block_state = mm("htd,hte->hde", keys_end, v)
    prev_state = split(two_level_sum(block_state, decay_rate, float(length), False, (chunk_first, chunks[0])))
    attn = (mm("htd,hsd->hts", q, k) * mask_decay).astype(BF16)
    inside = mm("hts,hse->hte", attn, v)
    attn_out = (inside + inner_weight * mm_split("htd,hde->hte", q, prev_state)).astype(BF16)

    flat_out = jnp.transpose(attn_out, (1, 0, 2)).reshape(length, heads_here * head_size)
    flat_out = reorder(flat_out, order)

    def gather_step(held, step):
        return [
            lax.ppermute(held[p], ("ctx", "head"), step_pairs(p, step)) for p in range(2)
        ]

    def joined(held, got):
        return [jnp.concatenate([held[p], got[p]], axis=0) for p in range(2)]

    def after(a, other):
        return lax.optimization_barrier((a, other))[0]

    held = [flat_out[:, :256], flat_out[:, 256:]]
    got = gather_step(held, 0)
    part, part_there = layer_product(after(flat_out, chunks[1]), out_weight)
    from_pair = swap(after(part_there, got))
    held = joined(held, got)
    got = gather_step(held, 1)
    chunk = after(chunk, got)
    quarter = lax.dynamic_slice_in_dim(chunk, core * 16, 16, axis=0)
    quarter = lax.ppermute(quarter, "head", SPREAD)
    held = joined(held, got)
    got = gather_step(held, 2)

    packed = pack_columns((*chunks, after(quarter, got), out_grad), n_col)
    packed_there = swap(packed)
    cols_here = lax.all_to_all(packed, "ctx", split_axis=0, concat_axis=0, tiled=True)
    held = joined(held, got)
    last = gather_step(held, 3)

    def partial_rows(start, size):
        rows = slice(start, start + size)
        return part[rows] + from_pair[rows].astype(F32)

    moving = lax.ppermute(partial_rows(96, 16).astype(BF16), "head", COLLECT)
    moved = [moving]
    moving = moving.astype(F32)
    zero = jnp.zeros_like(moving)
    moving = jnp.where(
        core == 0,
        jnp.concatenate([moving, zero], axis=0),
        jnp.concatenate([zero, moving], axis=0),
    )
    for at in (64, 32):
        moving = (moving + partial_rows(at, 32)).astype(BF16)
        moved.append(lax.ppermute(moving, "head", COLLECT))
        moving = moved[-1].astype(F32)

    packed_there = lax.optimization_barrier((packed_there, moved[0]))[0]
    g = grad_product(order.astype(jnp.int32), packed, packed_there, out_weight)

    masks = jnp.asarray(
        [[gather_masks(ORDERS[p][c]) for p in range(2)] for c in range(2)], jnp.int32
    )
    table = ctx.astype(jnp.int32) ^ jnp.where(core == 0, masks[0], masks[1])

    def weights(before):
        ours = after(cols_here, before)
        theirs = swap(ours)
        first = weight_product(table[:, :8], held, ours, theirs, None)
        return weight_product(table[:, 8:], last, ours, theirs, first)

    finished = []

    def while_last_level(total):
        chunk = after((moving + partial_rows(0, 32)).astype(BF16), total)
        finished.append(lax.ppermute(chunk, "head", COLLECT))
        return None

    queries_start = (q * start_weight).astype(BF16)
    grad_block = mm("htd,hte->hde", queries_start, g)
    next_grad = split(
        two_level_sum(
            grad_block, decay_rate, float(length), True, (moved[2], while_last_level), last
        )
    )
    weight_grad = weights(next_grad[0])
    moving = after(finished[0], next_grad[0])
    for_here = lax.dynamic_slice_in_dim(moving, core * 16, 16, axis=0)
    for_there = lax.dynamic_slice_in_dim(moving, (1 - core) * 16, 16, axis=0)
    layer_out = partial_rows(112, 16) + for_here.astype(F32) + swap(for_there).astype(F32)
    layer_out = layer_out.astype(BF16)

    grad_scores = (mm("hte,hse->hts", g, v) * mask_decay).astype(BF16)
    query_grad = mm("hts,hsd->htd", grad_scores, k) + inner_weight * mm_split(
        "hte,hde->htd", g, prev_state
    )
    key_grad = mm("hts,htd->hsd", grad_scores, q) + tail_weight * mm_split(
        "hse,hde->hsd", v, next_grad
    )
    value_grad = mm("hts,hte->hse", attn, g) + tail_weight * mm_split(
        "hsd,hde->hse", k, next_grad
    )

    def back(a):
        return jnp.transpose(a, (1, 0, 2)).astype(BF16)

    return (layer_out, back(query_grad), back(key_grad), back(value_grad), weight_grad)


def solution(mesh):
    return jax.shard_map(
        body,
        mesh=mesh,
        in_specs=(
            P("ctx", "head", None),
            P("ctx", "head", None),
            P("ctx", "head", None),
            P("head", None),
            P("head"),
            P(("ctx", "head"), None),
        ),
        out_specs=(
            P(("ctx", "head"), None),
            P("ctx", "head", None),
            P("ctx", "head", None),
            P("ctx", "head", None),
            P("head", "ctx"),
        ),
        check_vma=False,
    )
```

```python
import jax
import jax.numpy as jnp
from jax import lax
from jax.experimental import pallas as pl
from jax.experimental.pallas import tpu as pltpu
from jax.sharding import PartitionSpec as P

F32 = jnp.float32
BF16 = jnp.bfloat16
N_CTX = 16
N_Z = 8

CORE_PAIR = [(h, h ^ 1) for h in range(16)]
SPREAD = [(h, (h - 2 if h % 2 == 0 else h + 2) % 16) for h in range(16)]
COLLECT = [(h, (h + 2 if h % 2 == 0 else h - 2) % 16) for h in range(16)]
ORDERS = (((1, 3, 4, 12), (4, 12, 1, 3)), ((3, 1, 12, 4), (12, 4, 3, 1)))


def x_shift(d):
    return [(c, (c + 4 * d) % 16) for c in range(16)]


def y_shift(d):
    return [(c, (c // 4) * 4 + (c + d) % 4) for c in range(16)]


def step_pairs(pair, step):
    masks = [ORDERS[pair][core][step] for core in range(2)]
    return [
        (c * 16 + h, (c ^ masks[h % 2]) * 16 + h) for c in range(16) for h in range(16)
    ]


def gather_masks(order):
    masks = [0]
    for mask in order:
        masks = masks + [m ^ mask for m in masks]
    return masks


def two_level_sum(state, rate, length, reverse, ties):
    place = lax.axis_index("ctx")
    x, y = place // 4, place % 4
    sign = -1 if reverse else 1

    def power(n):
        return jnp.exp(-rate * (length * n.astype(F32)))[:, None, None]

    def ahead(at, d):
        return (at >= d) if not reverse else (at + d <= 3)

    def level(own, at, shift, scale, tie):
        sent = own.astype(BF16)
        got = [lax.ppermute(sent, "ctx", shift(sign * d)) for d in (1, 2, 3)]
        if tie is not None:
            got = lax.optimization_barrier((*got, tie))[:3]
        got = [part.astype(F32) for part in got]
        before = 0.0
        for d in (1, 2, 3):
            weight = jnp.where(ahead(at, d), power(jnp.asarray((d - 1) * scale)), 0.0)
            before = before + weight * got[d - 1]
        return before, got

    before_y, got = level(state, y, y_shift, 1, ties[0])
    to_end = (3 - y) if not reverse else y
    total = power(to_end) * state
    for d in (1, 2, 3):
        source = (y - sign * d) % 4
        left = (3 - source) if not reverse else source
        total = total + power(left) * got[d - 1]
    before_x, _ = level(total, x, x_shift, 4, ties[1])
    steps = y if not reverse else 3 - y
    return before_y + power(steps) * before_x


def weight_kernel(first, table, a0, a1, ours, theirs, *refs):
    out = refs[-1]
    for pair, part in enumerate((a0, a1)):
        rows = slice(pair * 256, (pair + 1) * 256)
        total = jnp.zeros((256, 384), F32) if first else refs[0][rows, :]
        for i in range(8):
            at = table[pair, i]
            block = jnp.concatenate([ours[at], theirs[at]], axis=0)
            total = total + lax.dot_general(
                part[i * 256 : (i + 1) * 256, :],
                block,
                (((0,), (0,)), ((), ())),
                preferred_element_type=F32,
            )
        out[rows, :] = total


def weight_product(table, parts, ours, theirs, earlier):
    first = earlier is None
    operands = list(parts) + [ours, theirs] + ([] if first else [earlier])
    return pl.pallas_call(
        lambda *refs: weight_kernel(first, *refs),
        out_shape=jax.ShapeDtypeStruct((512, 384), F32),
        in_specs=[pl.BlockSpec(memory_space=pltpu.SMEM)]
        + [pl.BlockSpec(memory_space=pltpu.VMEM)] * len(operands),
        out_specs=pl.BlockSpec(memory_space=pltpu.VMEM),
        compiler_params=pltpu.CompilerParams(vmem_limit_bytes=32 * 2**20),
        cost_estimate=pl.CostEstimate(
            flops=2 * 2048 * 512 * 384, bytes_accessed=6 * 2**20, transcendentals=0
        ),
    )(table, *operands)


def pack_kernel(c1, c2, c3, quarter, own, out):
    n_col = out.shape[2]
    row = 0
    for part in (c1, c2, c3, quarter, own):
        size = part.shape[0]
        for c in range(out.shape[0]):
            out[c, row : row + size, :] = part[:, c * n_col : (c + 1) * n_col]
        row += size


def pack_columns(parts, n_col):
    return pl.pallas_call(
        pack_kernel,
        out_shape=jax.ShapeDtypeStruct((N_CTX, 128, n_col), BF16),
        in_specs=[pl.BlockSpec(memory_space=pltpu.VMEM)] * 5,
        out_specs=pl.BlockSpec(memory_space=pltpu.VMEM),
        compiler_params=pltpu.CompilerParams(vmem_limit_bytes=16 * 2**20),
        cost_estimate=pl.CostEstimate(flops=0, bytes_accessed=3 * 2**20, transcendentals=0),
    )(*parts)


def grad_kernel(order, ours, theirs, weight, out, total):
    step = pl.program_id(0)

    @pl.when(step == 0)
    def _():
        total[...] = jnp.zeros_like(total)

    n_col = ours.shape[2]
    for c in range(ours.shape[0]):
        total[...] += lax.dot_general(
            jnp.concatenate([ours[c], theirs[c]], axis=0),
            weight[:, c * n_col : (c + 1) * n_col],
            (((1,), (1,)), ((), ())),
            preferred_element_type=F32,
        )

    @pl.when(step == pl.num_programs(0) - 1)
    def _():
        for piece in range(16):
            to = pl.ds(pl.multiple_of(order[piece] * 16, 16), 16)
            rows = total[piece * 16 : (piece + 1) * 16, :].astype(BF16)
            for j in range(4):
                out[j, to, :] = rows[:, j * 128 : (j + 1) * 128]


def grad_product(order, ours, theirs, weight):
    n_col = ours.shape[2]
    rows_spec = pl.BlockSpec((4, 128, n_col), lambda i: (i, 0, 0))
    return pl.pallas_call(
        grad_kernel,
        out_shape=jax.ShapeDtypeStruct((4, 256, 128), BF16),
        grid=(4,),
        in_specs=[pl.BlockSpec(memory_space=pltpu.SMEM), rows_spec, rows_spec, pl.BlockSpec((512, 4 * n_col), lambda i: (0, i))],
        out_specs=pl.BlockSpec((4, 256, 128), lambda i: (0, 0, 0)),
        scratch_shapes=[pltpu.VMEM((256, 512), F32)],
        compiler_params=pltpu.CompilerParams(vmem_limit_bytes=58 * 2**20),
        cost_estimate=pl.CostEstimate(
            flops=2 * 256 * 512 * 6144, bytes_accessed=10 * 2**20, transcendentals=0
        ),
    )(order, ours, theirs, weight)


def layer_kernel(flat, weight, ours, theirs):
    both = jnp.dot(flat[...], weight[...], preferred_element_type=F32)
    ours[...] = both[:128]
    theirs[...] = both[128:].astype(BF16)


def layer_product(flat, weight):
    width = weight.shape[1] // 4
    return pl.pallas_call(
        layer_kernel,
        out_shape=(
            jax.ShapeDtypeStruct((128, 4 * width), F32),
            jax.ShapeDtypeStruct((128, 4 * width), BF16),
        ),
        grid=(4,),
        in_specs=[
            pl.BlockSpec((256, 512), lambda i: (0, 0)),
            pl.BlockSpec((512, width), lambda i: (0, i)),
        ],
        out_specs=(
            pl.BlockSpec((128, width), lambda i: (0, i)),
            pl.BlockSpec((128, width), lambda i: (0, i)),
        ),
        compiler_params=pltpu.CompilerParams(vmem_limit_bytes=58 * 2**20),
        cost_estimate=pl.CostEstimate(
            flops=2 * 256 * 512 * 6144, bytes_accessed=11 * 2**20, transcendentals=0
        ),
    )(flat, weight)


def body(queries, keys, values, out_weight, decay_rate, out_grad):
    length, heads_here, head_size = queries.shape
    ctx = lax.axis_index("ctx")
    head = lax.axis_index("head")
    z, core = head // 2, head % 2
    n_col = out_grad.shape[1] // N_CTX

    sign = 1 - 2 * core

    def swap(a):
        return lax.ppermute(a, "head", CORE_PAIR)

    def half_order(of_core, s):
        pieces = []
        for k in (1, 2, 3):
            base = 2 * ((z + s * k) % 8)
            pieces += [base, base + 1]
        return pieces + [2 * ((z + 4) % 8) + of_core, 2 * z + of_core]

    order = jnp.stack(half_order(core, sign) + half_order(1 - core, -sign))
    def reorder(a, by):
        return jnp.take(a.reshape(16, 16, -1), by, axis=0, mode="clip").reshape(a.shape)

    other = swap(out_grad)
    chunk = jnp.where(
        core == 0,
        jnp.concatenate([out_grad, other], axis=0),
        jnp.concatenate([other, out_grad], axis=0),
    )
    chunk_first = chunk
    chunks = []
    for k in (1, 2, 3):
        chunk = lax.ppermute(chunk, "head", SPREAD)
        chunks.append(chunk)
    places = jnp.arange(length, dtype=F32)
    offsets = places[:, None] - places[None, :]
    mask_decay = jnp.where(
        offsets[None] >= 0,
        jnp.exp(-decay_rate[:, None, None] * jnp.maximum(offsets, 0.0)[None]),
        0.0,
    )

    def decay(n):
        return jnp.exp(-decay_rate[:, None] * n[None, :])[:, :, None]

    end_weight = decay(length - 1.0 - places)
    start_weight = decay(places)
    inner_weight = decay(places + 1.0)
    tail_weight = decay(length - places)

    q = jnp.transpose(queries, (1, 0, 2))
    k = jnp.transpose(keys, (1, 0, 2))
    v = jnp.transpose(values, (1, 0, 2))

    def mm(form, a, b):
        return jnp.einsum(form, a, b, preferred_element_type=F32)

    def split(a):
        high = a.astype(BF16)
        return high, (a - high.astype(F32)).astype(BF16)

    def mm_split(form, a, b):
        return mm(form, a, b[0]) + mm(form, a, b[1])

    keys_end = (k * end_weight).astype(BF16)
    block_state = mm("htd,hte->hde", keys_end, v)
    prev_state = split(two_level_sum(block_state, decay_rate, float(length), False, (chunk_first, chunks[0])))
    attn = (mm("htd,hsd->hts", q, k) * mask_decay).astype(BF16)
    inside = mm("hts,hse->hte", attn, v)
    attn_out = (inside + inner_weight * mm_split("htd,hde->hte", q, prev_state)).astype(BF16)

    flat_out = jnp.transpose(attn_out, (1, 0, 2)).reshape(length, heads_here * head_size)
    flat_out = reorder(flat_out, order)

    def gather_step(held, step):
        return [
            lax.ppermute(held[p], ("ctx", "head"), step_pairs(p, step)) for p in range(2)
        ]

    def joined(held, got):
        return [jnp.concatenate([held[p], got[p]], axis=0) for p in range(2)]

    def after(a, other):
        return lax.optimization_barrier((a, other))[0]

    held = [flat_out[:, :256], flat_out[:, 256:]]
    got = gather_step(held, 0)
    part, part_there = layer_product(after(flat_out, chunks[1]), out_weight)
    from_pair = swap(after(part_there, got))
    held = joined(held, got)
    got = gather_step(held, 1)
    chunk = after(chunk, got)
    quarter = lax.dynamic_slice_in_dim(chunk, core * 16, 16, axis=0)
    quarter = lax.ppermute(quarter, "head", SPREAD)
    held = joined(held, got)
    got = gather_step(held, 2)

    packed = pack_columns((*chunks, after(quarter, got), out_grad), n_col)
    packed_there = swap(packed)
    cols_here = lax.all_to_all(packed, "ctx", split_axis=0, concat_axis=0, tiled=True)
    held = joined(held, got)
    last = gather_step(held, 3)

    def partial_rows(start, size):
        rows = slice(start, start + size)
        return part[rows] + from_pair[rows].astype(F32)

    moving = lax.ppermute(partial_rows(96, 16).astype(BF16), "head", COLLECT)
    moved = [moving]
    moving = moving.astype(F32)
    zero = jnp.zeros_like(moving)
    moving = jnp.where(
        core == 0,
        jnp.concatenate([moving, zero], axis=0),
        jnp.concatenate([zero, moving], axis=0),
    )
    for at in (64, 32, 0):
        moving = (moving + partial_rows(at, 32)).astype(BF16)
        moved.append(lax.ppermute(moving, "head", COLLECT))
        moving = moved[-1].astype(F32)
    moving = moved[-1]
    for_here = lax.dynamic_slice_in_dim(moving, core * 16, 16, axis=0)
    for_there = lax.dynamic_slice_in_dim(moving, (1 - core) * 16, 16, axis=0)
    layer_out = partial_rows(112, 16) + for_here.astype(F32) + swap(for_there).astype(F32)
    layer_out = layer_out.astype(BF16)

    packed_there = lax.optimization_barrier((packed_there, moved[0]))[0]
    g = grad_product(order.astype(jnp.int32), packed, packed_there, out_weight)

    cols_here = lax.optimization_barrier((cols_here, g))[0]
    cols_there = swap(cols_here)

    queries_start = (q * start_weight).astype(BF16)
    grad_block = mm("htd,hte->hde", queries_start, g)
    next_grad = split(two_level_sum(grad_block, decay_rate, float(length), True, ((moved[2], last), moved[3])))
    grad_scores = (mm("hte,hse->hts", g, v) * mask_decay).astype(BF16)
    query_grad = mm("hts,hsd->htd", grad_scores, k) + inner_weight * mm_split(
        "hte,hde->htd", g, prev_state
    )
    key_grad = mm("hts,htd->hsd", grad_scores, q) + tail_weight * mm_split(
        "hse,hde->hsd", v, next_grad
    )
    value_grad = mm("hts,hte->hse", attn, g) + tail_weight * mm_split(
        "hsd,hde->hse", k, next_grad
    )

    masks = jnp.asarray(
        [[gather_masks(ORDERS[p][c]) for p in range(2)] for c in range(2)], jnp.int32
    )
    table = ctx.astype(jnp.int32) ^ jnp.where(core == 0, masks[0], masks[1])
    weight_grad = weight_product(table[:, :8], held, cols_here, cols_there, None)
    weight_grad = weight_product(table[:, 8:], last, cols_here, cols_there, weight_grad)

    def back(a):
        return jnp.transpose(a, (1, 0, 2)).astype(BF16)

    return (layer_out, back(query_grad), back(key_grad), back(value_grad), weight_grad)


def solution(mesh):
    return jax.shard_map(
        body,
        mesh=mesh,
        in_specs=(
            P("ctx", "head", None),
            P("ctx", "head", None),
            P("ctx", "head", None),
            P("head", None),
            P("head"),
            P(("ctx", "head"), None),
        ),
        out_specs=(
            P(("ctx", "head"), None),
            P("ctx", "head", None),
            P("ctx", "head", None),
            P("ctx", "head", None),
            P("head", "ctx"),
        ),
        check_vma=False,
    )
```
